32 devices in a mesh: batch: 8 (over y, x, core), tensor: 4 (over z).
Axes of the slice: x: 2, y: 2, z: 4, core: 2. Of those that a mesh axis runs over, the one named last changes fastest.
Arguments:
- inputs: bfloat16 [1024, 16, 768], P('tensor', 'batch'), may hold values from -6 to 6
- lengths: int32 [16], P('batch'), may hold values from 128 to 1024, as said below
- gain_one: bfloat16 [768], replicated, may hold values from 0.25 to 1.75
- qkv_weight: bfloat16 [3, 768, 768], P(None, None, 'tensor'), may hold values from -0.3125 to 0.3125
- out_weight: bfloat16 [768, 768], P('tensor'), may hold values from -2.5 to 2.5
- gain_two: bfloat16 [768], replicated, may hold values from 0.25 to 1.75
- up_projection_weight: bfloat16 [768, 3072], P(None, 'tensor'), may hold values from -0.21875 to 0.21875
- down_projection_weight: bfloat16 [3072, 768], P('tensor'), may hold values from -0.109375 to 0.109375
- pair_bias: float32 [1024, 512], replicated, may hold values from -3 to 3
- cotangent: bfloat16 [1024, 16, 768], P('tensor', 'batch'), may hold values from -6 to 6
Outputs:
- mixed: bfloat16 [1024, 16, 768], P('tensor', 'batch')
- grad_inputs: float32 [1024, 16, 768], P('tensor', 'batch')
- grad_gain_one: float32 [768], replicated
- grad_qkv: float32 [3, 768, 768], P(None, None, 'tensor')
- grad_out: float32 [768, 768], P('tensor')
- grad_gain_two: float32 [768], replicated
- up_weight_gradient: float32 [768, 3072], P(None, 'tensor')
- down_weight_gradient: float32 [3072, 768], P('tensor')
- grad_pair: float32 [1024, 512], replicated
The draws below stay inside these ranges and needn't reach their ends.
Inputs may be any that keep to these rules, and one draw needn't show every extreme that they name: `lengths`: each length is a multiple of 128; among the 2 rows of each index of batch at least one, drawn from the seed, has length 1024.
All inputs are finite; a program needn't handle non-finite values.
Results may differ from the reference program's by a relative error of at most 0.017.
Values may be sent and summed in bfloat16 or wider, within the bound.
A program may use at most 192 MiB of HBM per device.

```python
import jax
import jax.numpy as jnp
from jax import lax

D = 768
FF = 3072
LMAX = 1024
WIN = 256
R_DEV = 2
ROWS = 16


def draw_lengths(key, part):
    first_key, second_key, third_key = jax.random.split(key, 3)
    first_draw = jax.random.randint(first_key, (ROWS,), 1, 9)
    second_draw = jax.random.randint(second_key, (ROWS,), 1, 9)
    bucket = jnp.minimum(first_draw, second_draw)
    bucketed = bucket * (LMAX // 8)
    selected_rows = jax.random.randint(third_key, (ROWS // R_DEV,), 0, R_DEV)
    full_row = jnp.arange(ROWS) % R_DEV == jnp.repeat(selected_rows, R_DEV)
    return jnp.where(full_row, LMAX, bucketed).astype(jnp.int32)


def levels(own_key, shape, shards, smallest, top_value):
    loudness = 1.0
    for position, parts in shards:
        steps = jax.random.uniform(jax.random.fold_in(jax.random.fold_in(own_key, 6), position), (parts,), jnp.float32, smallest / len(shards), top_value / len(shards))
        loudness = loudness * jnp.repeat(jnp.exp(steps), shape[position] // parts).reshape((-1,) + (1,) * (len(shape) - 1 - position))
    return loudness


def scatter_about(rng, shape, deviation, limit, cuts=(), held_as=jnp.bfloat16):
    array = deviation * jax.random.normal(rng, shape, jnp.float32)
    if cuts:
        array = array * levels(rng, shape, cuts, -0.22, 0.18)
    return jnp.clip(array, -limit, limit).astype(held_as)


def setup_inputs(seed: int = 0) -> dict:
    keys = jax.random.split(jax.random.key(seed), 11)
    return {
        "inputs": scatter_about(keys[0], (LMAX, ROWS, D), 1.0, 6.0, ((0, 4), (1, 8))),
        "lengths": draw_lengths(jax.random.fold_in(keys[10], 71), 0),
        "gain_one": jnp.clip(1.0 + 0.15 * jax.random.normal(keys[2], (D,), jnp.float32), 0.25, 1.75).astype(jnp.bfloat16),
        "qkv_weight": scatter_about(keys[3], (3, D, D), (D // 2) ** -0.5, 0.3125, ((2, 4),)),
        "out_weight": scatter_about(keys[4], (D, D), (max(D // 128, 1)) ** -0.5, 2.5, ((0, 4),)),
        "gain_two": jnp.clip(1.0 + 0.15 * jax.random.normal(keys[5], (D,), jnp.float32), 0.25, 1.75).astype(jnp.bfloat16),
        "up_projection_weight": scatter_about(keys[6], (D, FF), D ** -0.5, 0.21875, ((1, 4),)),
        "down_projection_weight": scatter_about(keys[7], (FF, D), FF ** -0.5, 0.109375, ((0, 4),)),
        "pair_bias": scatter_about(keys[8], (LMAX, 2 * WIN), 0.7, 3.0, (), jnp.float32),
        "cotangent": scatter_about(keys[9], (LMAX, ROWS, D), 1.0, 6.0, ((0, 4), (1, 8))),
    }


@jax.custom_vjp
def low(v):
    return lax.optimization_barrier(v.astype(jnp.bfloat16)).astype(jnp.float32)

@jax.custom_vjp
def low_back(v):
    return v

def low_keep(v):
    return (low(v), None)

def low_pass(kept, grad):
    return (grad,)

def back_keep(v):
    return (v, None)

def back_low(kept, grad):
    return (low(grad),)
low.defvjp(low_keep, low_pass)
low_back.defvjp(back_keep, back_low)

def layer_norm(values, gain):
    center = lax.optimization_barrier(jnp.mean(values, axis=-1, keepdims=True))
    shifted = values - center
    spread = lax.optimization_barrier(jnp.mean(shifted * shifted, axis=-1, keepdims=True))
    return shifted * lax.rsqrt(spread + 1e-05) * gain

def gelu_tanh(values):
    return jax.nn.gelu(values, approximate=True)

def band_full(pair_bias):
    length, doubled = pair_bias.shape
    half = doubled // 2
    padded = jnp.pad(pair_bias, ((0, 0), (0, length + 1)))
    flat = padded.reshape(-1)[:length * (length + doubled)]
    placed = flat.reshape(length, length + doubled)[:, half:half + length]
    offset = jnp.arange(length)[None, :] - jnp.arange(length)[:, None]
    inside = (offset >= -half) & (offset < half)
    return jnp.where(inside, jnp.exp(placed), 1.0)

def reference(inputs, lengths, gain_one, qkv_weight, out_weight, gain_two, up_projection_weight, down_projection_weight, pair_bias, cotangent):
    highest_precision = lax.Precision.HIGHEST
    length = inputs.shape[0]
    groups = inputs.shape[1] // 4
    row_lengths = lengths.reshape(groups, 4)

    def forward(inputs_float, gain_a, qkv_w, out_w, gain_b, up_matrix, down_matrix, bias_w):
        band_low = low(band_full(bias_w))
        stacked = jnp.transpose(inputs_float.reshape(length, groups, 4, D), (1, 0, 2, 3))

        def one_group(packed):
            row_block, group_lengths = packed
            normed_one = low(layer_norm(row_block, gain_a))
            projected = jnp.einsum('trd,kdc->ktrc', normed_one, qkv_w, precision=highest_precision)
            queries = low_back(projected[0])
            key_part = low_back(projected[1])
            values = low_back(projected[2])
            positions = jnp.arange(length)
            keep_mask = (positions[:, None] < group_lengths[None, :]).astype(jnp.float32)
            weights_exp = keep_mask[:, :, None] * jnp.exp(key_part)
            pairs = jnp.concatenate([low(weights_exp * values), low(weights_exp)], axis=-1)
            sums = low_back(jnp.einsum('ts,src->trc', band_low, pairs, precision=highest_precision))
            numer = sums[..., :D]
            denom = sums[..., D:]
            gates = jax.nn.sigmoid(queries)
            mixer = low(gates * numer / denom)
            branch = low_back(jnp.einsum('trc,cd->trd', mixer, out_w, precision=highest_precision))
            middle = row_block + branch
            second_normalized = low(layer_norm(middle, gain_b))
            hidden_state = low_back(jnp.einsum('eaj,jy->eay', second_normalized, up_matrix, precision=highest_precision))
            active_rows = low(gelu_tanh(hidden_state))
            second_branch = low_back(jnp.einsum('qoa,aj->qoj', active_rows, down_matrix, precision=highest_precision))
            return middle + second_branch
        results = lax.map(jax.checkpoint(one_group), (stacked, row_lengths))
        return jnp.transpose(results, (1, 0, 2, 3)).reshape(length, groups * 4, D)
    params = (inputs.astype(jnp.float32), gain_one.astype(jnp.float32), qkv_weight.astype(jnp.float32), out_weight.astype(jnp.float32), gain_two.astype(jnp.float32), up_projection_weight.astype(jnp.float32), down_projection_weight.astype(jnp.float32), pair_bias.astype(jnp.float32))
    result, pullback = jax.vjp(forward, *params)
    grads = pullback(cotangent.astype(jnp.float32))
    return (result.astype(jnp.bfloat16), grads[0], grads[1], grads[2], grads[3], grads[4], grads[5], grads[6], grads[7])
```

```python
import functools

import jax
import jax.numpy as jnp
from jax import lax
from jax.experimental import pallas as pl
from jax.experimental.pallas import tpu as pltpu
from jax.sharding import PartitionSpec as P

MESH = pl.DeviceIdType.MESH
BF = jnp.bfloat16
F32 = jnp.float32
GELU_A = 0.044715
GELU_C = 0.7978845608028654
VMEM_BYTES = 63 << 20


def dot(a, b, ca, cb):
    return lax.dot_general(a, b, (((ca,), (cb,)), ((), ())), preferred_element_type=F32)


def nn(a, b):
    return dot(a, b, 1, 0)


def nt(a, b):
    return dot(a, b, 1, 1)


def tn(a, b):
    return dot(a, b, 0, 0)


def norm_parts(v):
    shifted = v - jnp.mean(v, axis=-1, keepdims=True)
    rstd = lax.rsqrt(jnp.mean(shifted * shifted, axis=-1, keepdims=True) + 1e-05)
    return shifted * rstd, rstd


def kernel(
    tiles,
    bits,
    length,
    n_sems,
    len_ref,
    x_ref,
    cot_ref,
    gain1_ref,
    gain2_ref,
    w0_in,
    w1_in,
    w2_in,
    bias_in,
    mixed_ref,
    gin_ref,
    gains_ref,
    f_out,
    fp_out,
    W0,
    W1,
    W2,
    G1,
    G2,
    R1,
    R2,
    n1,
    pairs,
    gates,
    ratio,
    dinv,
    mid,
    act,
    n2,
    mix,
    gs,
    gn2,
    hr,
    band,
    GP,
    RP,
    FP,
    CS,
    CSR,
    far,
    GA,
    GR,
    UPP,
    ssem,
    rsem,
    lsem,
    ready,
    upper_ready,
):
    T = tiles
    rows, tile, depth = cot_ref.shape
    piece = W1.shape[4]
    half = piece // 2
    b = lax.axis_index("batch")
    z = lax.axis_index("tensor")
    c = lax.rem(b, 2)
    x = lax.rem(b // 2, 2)
    y = lax.rem(b // 4, 2)
    gh = mixed_ref

    def flip(k):
        q = lax.rem(b // (1 << k), 2)
        return (b + (1 << k) - 2 * (1 << k) * q, z)

    core, xp, yp = flip(0), flip(1), flip(2)
    counter = [0]

    def take(n):
        counter[0] += n
        assert counter[0] <= n_sems
        return counter[0] - n

    def rc(src, dst, sem, dev):
        return pltpu.make_async_remote_copy(
            src_ref=src,
            dst_ref=dst,
            send_sem=ssem.at[sem],
            recv_sem=rsem.at[sem],
            device_id=dev,
            device_id_type=MESH,
        )

    def slab(i):
        return lax.rem(z + i, T)

    lo, hi = pl.ds(0, half), pl.ds(half, half)
    partners = [flip(k) for k in range(bits)] + [(b, slab(i)) for i in range(1, T)]

    def w_at(g, j):
        return W0.at[:, :, j] if g == 0 else (W1, W2)[g - 1].at[j]

    w_in = (w0_in, w1_in, w2_in)
    local = [pltpu.make_async_copy(w_in[g], w_at(g, z), lsem.at[g]) for g in range(3)]
    window = bias_in.shape[1]
    bias = gn2.at[0, :, pl.ds(0, window)]
    local.append(pltpu.make_async_copy(bias_in.at[pl.ds(z * tile, tile)], bias, lsem.at[3]))
    local.append(pltpu.make_async_copy(x_ref, n1.at[:, 1], lsem.at[4]))
    for cp in local:
        cp.start()

    barrier = pltpu.get_barrier_semaphore()
    for dev in partners:
        pl.semaphore_signal(barrier, inc=1, device_id=dev, device_id_type=MESH)
    pl.semaphore_wait(barrier, len(partners))

    z_base, a1_base, a2_base, a3_base = take(3 * T), take(6 * T), take(6 * T), take(3 * T)

    def ag_z(g, i):
        dst = W0.at[y, x, z, c] if g == 0 else (W1, W2)[g - 1].at[z, y, x, c]
        return rc(w_in[g].at[y, x, c], dst, z_base + g * T + i, (b, slab(i)))

    def ag_1(g, i, h):
        j = slab(T - i)
        rng = (lo, hi)[h]
        ref = W0.at[y, x, j, c, rng] if g == 0 else (W1, W2)[g - 1].at[j, y, x, c, rng]
        return rc(ref, ref, a1_base + (g * 2 + h) * T + i, (xp, yp)[h])

    def ag_2(g, i, h):
        j = slab(T - i)
        W = (W0, W1, W2)[g]
        if h == 0:
            ref = W.at[y, :, j, c, lo] if g == 0 else W.at[j, y, :, c, lo]
        else:
            ref = W.at[:, x, j, c, hi] if g == 0 else W.at[j, :, x, c, hi]
        return rc(ref, ref, a2_base + (g * 2 + h) * T + i, (yp, xp)[h])

    def ag_3(g, i):
        j = slab(T - i)
        ref = W0.at[:, :, j, c] if g == 0 else (W1, W2)[g - 1].at[j, :, :, c]
        return rc(ref, ref, a3_base + g * T + i, core)

    others = range(1, T)

    def ag_start_z(g):
        for i in others:
            ag_z(g, i).start()

    def ag_step_1(g):
        for i in others:
            ag_z(g, i).wait()
            for h in range(2):
                ag_1(g, i, h).start()

    def ag_step_2(g):
        for i in others:
            for h in range(2):
                ag_1(g, i, h).wait()
                ag_2(g, i, h).start()

    def ag_step_3(g):
        for i in others:
            for h in range(2):
                ag_2(g, i, h).wait()
            ag_3(g, i).start()

    def ag_end(g):
        for i in others:
            ag_3(g, i).wait()

    halo_base = take(4)

    def halo_right():
        return rc(x_ref, n1.at[:, 0], halo_base, (b, lax.min(z + 1, T - 1)))

    def halo_left():
        return rc(x_ref, n1.at[:, 2], halo_base + 1, (b, lax.max(z - 1, 0)))

    ag_start_z(0)
    pl.when(z < T - 1)(lambda: halo_right().start())
    pl.when(z > 0)(lambda: halo_left().start())

    @pl.when(z == 0)
    def _():
        n1[:, 0] = jnp.zeros((rows, tile, depth), BF)
        hr[0] = jnp.zeros((rows, tile, depth), BF)

    @pl.when(z == T - 1)
    def _():
        n1[:, 2] = jnp.zeros((rows, tile, depth), BF)
        hr[1] = jnp.zeros((rows, tile, depth), BF)

    gain1 = gain1_ref[...]
    gain2 = gain2_ref[...]

    def loop(n, body):
        def step(i, carry):
            body(i)
            return carry

        lax.fori_loop(0, n, step, 0)

    def norm_tile(r, t):
        xhat, _ = norm_parts(n1[r, t].astype(F32))
        n1[r, t] = (xhat * gain1).astype(BF)

    local[3].wait()
    wide = jnp.concatenate([jnp.exp(bias[...]), jnp.ones((tile, 3 * tile - window), F32)], axis=1)
    band[...] = pltpu.roll(wide, 0, 1, stride=1, stride_axis=0).astype(BF)
    local[4].wait()
    loop(rows, lambda r: norm_tile(r, 1))

    def mat(ref):
        return ref[...].reshape(depth, depth)

    Wq, Wk, Wv, Wo = W0.at[0, 0], W0.at[0, 1], W0.at[1, 0], W0.at[1, 1]

    ag_step_1(0)
    ag_start_z(1)
    ag_step_2(0)
    ag_step_3(0)
    ag_step_1(1)
    ag_start_z(2)
    ag_end(0)
    local[0].wait()

    def key_values(r, t):
        n = n1[r, t]
        pos = (z - 1 + t) * tile + lax.broadcasted_iota(jnp.int32, (tile, 1), 0)
        keep = (pos >= 0) & (pos < length) & (pos < len_ref[r])
        e = jnp.where(keep, jnp.exp(nt(n, mat(Wk))), 0.0)
        v = nt(n, mat(Wv))
        pairs[r, t, :, pl.ds(0, depth)] = (e * v).astype(BF)
        pairs[r, t, :, pl.ds(depth, depth)] = e.astype(BF)

    def own_qkv(r):
        gates[r] = jax.nn.sigmoid(nt(n1[r, 1], mat(Wq)))
        key_values(r, 1)

    loop(rows, own_qkv)
    ag_step_2(1)

    ones = jnp.ones((8, tile), BF)
    row_of = lax.broadcasted_iota(jnp.int32, (8, 1), 0)
    cs_base = take(2 * T)

    def cs_send(k, i):
        return rc(CS.at[k], CSR.at[k, i - 1], cs_base + k * T + i, (b, slab(i)))

    def cs_start(k, first, second):
        CS[k] = jnp.where(row_of == 0, first, second)
        for i in others:
            cs_send(k, i).start()

    def cs_finish(k):
        total = jnp.zeros(far.shape[1:], F32)
        for i in others:
            cs_send(k, i).wait()
            distance = lax.abs(lax.rem(z - i + T, T) - z)
            total = total + jnp.where(distance >= 2, CSR[k, i - 1], 0.0)
        far[k] = total

    cs_start(0, nn(ones, pairs[0, 1]), nn(ones, pairs[1, 1]))

    pl.when(z < T - 1)(lambda: halo_right().wait_send())
    pl.when(z > 0)(lambda: halo_left().wait_send())
    pl.when(z > 0)(lambda: halo_right().wait_recv())
    pl.when(z < T - 1)(lambda: halo_left().wait_recv())

    def halo_kv(i):
        r = lax.rem(i, rows)
        t = 2 * (i // rows)
        norm_tile(r, t)
        key_values(r, t)

    loop(2 * rows, halo_kv)
    ag_step_3(1)
    ag_step_1(2)
    cs_finish(0)

    x_again = pltpu.make_async_copy(x_ref, act, lsem.at[4])
    x_again.start()

    def mixer(r):
        denom = nn(band[...], pairs[r, :, :, pl.ds(depth, depth)].reshape(3 * tile, depth))
        denom = denom + far[0, pl.ds(r, 1), pl.ds(depth, depth)]
        di = 1.0 / denom
        dinv[r] = di
        numer = nn(band[...], pairs[r, :, :, pl.ds(0, depth)].reshape(3 * tile, depth))
        rt = (numer + far[0, pl.ds(r, 1), pl.ds(0, depth)]) * di
        ratio[r] = rt
        mix[r] = (gates[r] * rt).astype(BF)

    loop(rows, mixer)
    ag_step_2(2)
    x_again.wait()

    def middle(r):
        m = act[r].astype(F32) + nn(mix[r], mat(Wo))
        mid[r] = m
        gin_ref[r] = m
        xhat, _ = norm_parts(m)
        n2[r] = (xhat * gain2).astype(BF)
        gn2[r] = jnp.zeros((tile, depth), F32)

    loop(rows, middle)
    ag_end(1)
    ag_step_3(2)
    local[1].wait()
    local[2].wait()
    ag_end(2)

    G = (W1, G1, G2)
    R = (W2, R1, R2)
    s1_base, s2_base, s3_base, sz_base, f_base = take(3 * 4), take(6 * T), take(6 * T), take(3 * T), take(15)

    def s1(g, i):
        j = slab(i + 1)
        return rc(G[g].at[j, :, :, 1 - c], R[g].at[j, :, :, 0], s1_base + g * 4 + i, core)

    def s1_kind(ty, tx):
        return rc(G[0].at[:, ty, tx, 1 - c], R[0].at[:, ty, tx, 0], s1_base + 2 * ty + tx, core)

    def s2(g, i, h):
        j = slab(i + 1)
        if h == 0:
            src, dst, dev = G[g].at[j, :, 1 - x, c, lo], R[g].at[j, 0, :, 1, lo], xp
        else:
            src, dst, dev = G[g].at[j, 1 - y, :, c, hi], R[g].at[j, 0, :, 1, hi], yp
        return rc(src, dst, s2_base + (g * 2 + h) * T + i, dev)

    def s3(g, i, h):
        j = slab(i + 1)
        if h == 0:
            src, dst, dev = G[g].at[j, 1 - y, x, c, lo], R[g].at[j, 1, 0, 1, lo], yp
        else:
            src, dst, dev = G[g].at[j, y, 1 - x, c, hi], R[g].at[j, 1, 0, 1, hi], xp
        return rc(src, dst, s3_base + (g * 2 + h) * T + i, dev)

    def sz(g, i):
        return rc(G[g].at[slab(i + 1), y, x, c], R[g].at[i, 1, 1, 1], sz_base + g * T + i, (b, slab(i + 1)))

    def add_s1(g, i):
        j = slab(i + 1)
        G[g][j, :, :, c] = G[g][j, :, :, c] + R[g][j, :, :, 0]
        for h in range(2):
            s2(g, i, h).start()

    def s1_finish(g, i):
        s1(g, i).wait()
        add_s1(g, i)

    def s2_finish(g, i):
        j = slab(i + 1)
        s2(g, i, 0).wait()
        G[g][j, :, x, c, lo] = G[g][j, :, x, c, lo] + R[g][j, 0, :, 1, lo]
        s3(g, i, 0).start()
        s2(g, i, 1).wait()
        G[g][j, y, :, c, hi] = G[g][j, y, :, c, hi] + R[g][j, 0, :, 1, hi]
        s3(g, i, 1).start()

    def s3_finish(g, i):
        j = slab(i + 1)
        s3(g, i, 0).wait()
        s3(g, i, 1).wait()
        G[g][j, y, x, c] = G[g][j, y, x, c] + R[g][j, 1, 0, 1]
        if i < T - 1:
            sz(g, i).start()

    def f_at(g):
        return G[g].at[:, :, :, 1 - c]

    def f1(g, h):
        rng = (lo, hi)[h]
        other = f_at(g).at[c, y, x, rng]
        return rc(other, other, f_base + 5 * g + h, (xp, yp)[h])

    def f2(g, h):
        ref = f_at(g).at[c, y, :, lo] if h == 0 else f_at(g).at[c, :, x, hi]
        return rc(ref, ref, f_base + 5 * g + 2 + h, (yp, xp)[h])

    def f3(g):
        return rc(f_at(g).at[c], G[g].at[c, :, :, c], f_base + 5 * g + 4, core)

    u_base = take(4 * max(bits - 3, 0))

    def z_finish(g):
        total = G[g][z, y, x, c].astype(F32)
        for i in range(T - 1):
            sz(g, i).wait()
            total = total + R[g][i, 1, 1, 1].astype(F32)
        mine = f_at(g).at[c, y, x]
        mine[...] = total.astype(BF)
        for k in range(3, bits):
            u = k - 3
            slot = f_at(g).at[2 + u // 4, u // 2 % 2, u % 2]
            pl.semaphore_signal(upper_ready.at[g, u], inc=1, device_id=flip(k), device_id_type=MESH)
            pl.semaphore_wait(upper_ready.at[g, u], 1)
            cp = rc(mine, slot, u_base + g * (bits - 3) + u, flip(k))
            cp.start()
            cp.wait()
            mine[...] = mine[...] + slot[...]
        for h in range(2):
            f1(g, h).start()

    def f1_finish(g):
        for h in range(2):
            f1(g, h).wait()
            f2(g, h).start()

    def f2_finish(g):
        for h in range(2):
            f2(g, h).wait()
        f3(g).start()

    def out_copy(g, k):
        src = G[g].at[k, :, :, 1 - c]
        return pltpu.make_async_copy(src, f_out.at[g, :, :, k], lsem.at[5 + 2 * g + k])

    def f3_finish(g):
        f3(g).wait()
        for k in range(2):
            out_copy(g, k).start()

    def feed(i):
        j = slab(i + 1)
        up, down = W1.at[j], W2.at[j]

        def part(r):
            for k in range(3):
                cols = pl.ds(k * (depth // 3), depth // 3)
                h = nn(n2[r], up[:, :, :, :, cols].reshape(depth, depth // 3))
                ga = nt(cot_ref[r], down[...].reshape(depth, depth)[k * (depth // 3) : (k + 1) * (depth // 3)])
                sq = h * h
                t = jnp.tanh(GELU_C * h * (1.0 + GELU_A * sq))
                hh = 0.5 * h
                act[r, :, cols] = (hh + hh * t).astype(BF)
                slope = 0.5 + 0.5 * t + hh * (1.0 - t * t) * (GELU_C + (3.0 * GELU_C * GELU_A) * sq)
                gh[r, :, cols] = (ga * slope).astype(BF)
            gin_ref[r] += nn(act[r], mat(down))
            gn2[r] += nt(gh[r], mat(up))

        loop(rows, part)
        for m in range(2):
            cols = pl.ds(m * (depth // 2), depth // 2)
            d = tn(act[:, :, cols].reshape(rows * tile, depth // 2), cot_ref[...].reshape(rows * tile, depth))
            G2[j, m] = d.astype(BF).reshape(2, 2, piece, depth)
            d = tn(n2[:, :, cols].reshape(rows * tile, depth // 2), gh[...].reshape(rows * tile, depth))
            G1[j, m] = d.astype(BF).reshape(2, 2, piece, depth)
        s1(1, i).start()
        s1(2, i).start()

        @pl.when(i > 0)
        def _():
            s1_finish(1, i - 1)
            s1_finish(2, i - 1)

    loop(T, feed)
    for dev in partners:
        pl.semaphore_signal(ready, inc=1, device_id=dev, device_id_type=MESH)
    s1_finish(1, T - 1)
    s1_finish(2, T - 1)

    def norm_two_back(r, carry):
        mixed_ref[r] = gin_ref[r].astype(BF)
        xhat, rstd = norm_parts(mid[r])
        grad = gn2[r]
        carry = carry + jnp.sum(grad * xhat, axis=0, keepdims=True)
        g = grad * gain2
        back = g - jnp.mean(g, axis=-1, keepdims=True) - xhat * jnp.mean(g * xhat, axis=-1, keepdims=True)
        gm = cot_ref[r].astype(F32) + rstd * back
        mid[r] = gm
        n2[r] = gm.astype(BF)
        return carry

    gain2_grad = lax.fori_loop(0, rows, norm_two_back, jnp.zeros((1, depth), F32))

    for i in range(T):
        s2_finish(1, i)
        s2_finish(2, i)
    pl.semaphore_wait(ready, len(partners))

    local[3].start()

    def kind(ty, tx, lhs, start, rhs):
        for m in range(2):
            part = lhs[..., pl.ds(start + m * (depth // 2), depth // 2)]
            d = tn(part.reshape(rhs.shape[0], depth // 2), rhs).astype(BF)
            d = d.reshape(2, 2, piece, depth)
            for s in range(2):
                G[0][2 * m + s, ty, tx] = d[s]
        s1_kind(ty, tx).start()

    flat = (rows * tile, depth)
    kind(1, 1, mix, 0, n2[...].reshape(flat))

    def mixer_back(r):
        gmix = nt(n2[r], mat(Wo))
        gate = gates[r]
        rt = ratio[r]
        first = gmix * gate
        act[r] = (first * rt * (1.0 - gate)).astype(BF)
        first = first * dinv[r]
        gs[r, :, pl.ds(0, depth)] = first.astype(BF)
        gs[r, :, pl.ds(depth, depth)] = (-first * rt).astype(BF)

    loop(rows, mixer_back)
    cs_start(1, nn(ones, gs[0]), nn(ones, gs[1]))
    kind(0, 0, act, 0, n1[:, 1].reshape(flat))

    for i in range(T):
        s3_finish(1, i)
        s3_finish(2, i)

    local[3].wait()
    gband = nt(gs[0], pairs[0].reshape(3 * tile, 2 * depth)) + nt(gs[1], pairs[1].reshape(3 * tile, 2 * depth))
    shift = lax.broadcasted_iota(jnp.int32, (tile, 1), 0)
    k = 1
    while k < tile:
        gband = jnp.where(lax.rem(shift // k, 2) == 1, pltpu.roll(gband, 3 * tile - k, 1), gband)
        k *= 2
    gp = (gband[:, :window] * jnp.exp(bias[...])).astype(BF)
    GP[...] = gp.reshape(GP.shape)
    p_base = take(6 + T)
    up_base = u_base + 3 * max(bits - 3, 0)

    def p1():
        return rc(GP.at[:, :, 1 - c], RP.at[:, :, 0], p_base, core)

    def p2():
        return rc(GP.at[:, 1 - x, c], RP.at[0, :, 1], p_base + 1, xp)

    def p3():
        return rc(GP.at[1 - y, x, c], RP.at[1, 0, 1], p_base + 2, yp)

    def pz(i):
        mine = FP.at[z, y, x, c]
        return rc(mine, mine, p_base + 6 + i, (b, slab(i)))

    def pa1():
        ref = FP.at[:, y, x, c]
        return rc(ref, ref, p_base + 3, xp)

    def pa2():
        ref = FP.at[:, y, :, c]
        return rc(ref, ref, p_base + 4, yp)

    def pa3():
        ref = FP.at[:, :, :, c]
        return rc(ref, ref, p_base + 5, core)

    p1().start()
    z_finish(1)
    z_finish(2)
    cs_finish(1)

    def pairs_back(r):
        for t in range(3):
            near = band[:, pl.ds(t * tile, tile)]
            gn = tn(near, gs[r, :, pl.ds(0, depth)])
            gd = tn(near, gs[r, :, pl.ds(depth, depth)])
            if t == 1:
                gn = gn + far[1, pl.ds(r, 1), pl.ds(0, depth)]
                gd = gd + far[1, pl.ds(r, 1), pl.ds(depth, depth)]
            wv = pairs[r, t, :, pl.ds(0, depth)].astype(F32)
            we = pairs[r, t, :, pl.ds(depth, depth)].astype(F32)
            pairs[r, t, :, pl.ds(0, depth)] = (gn * wv + gd * we).astype(BF)
            pairs[r, t, :, pl.ds(depth, depth)] = (gn * we).astype(BF)

    loop(rows, pairs_back)
    p1().wait()
    GP[:, :, c] = GP[:, :, c] + RP[:, :, 0]
    p2().start()

    n1_all = n1[...].reshape(3 * rows * tile, depth)
    kind(0, 1, pairs, 0, n1_all)
    f1_finish(1)
    f1_finish(2)
    kind(1, 0, pairs, depth, n1_all)
    p2().wait()
    GP[:, x, c] = GP[:, x, c] + RP[0, :, 1]
    p3().start()
    for ty in range(2):
        for tx in range(2):
            s1_kind(ty, tx).wait()
    for i in range(T):
        add_s1(0, i)

    def halo_part(d):
        def body(r):
            g = nn(pairs[r, 2 * d, :, pl.ds(0, depth)], mat(Wk))
            g = g + nn(pairs[r, 2 * d, :, pl.ds(depth, depth)], mat(Wv))
            gs[r, :, pl.ds(d * depth, depth)] = g.astype(BF)

        loop(rows, body)

    def back_left():
        return rc(gs.at[:, :, pl.ds(0, depth)], hr.at[1], halo_base + 2, (b, lax.max(z - 1, 0)))

    def back_right():
        return rc(gs.at[:, :, pl.ds(depth, depth)], hr.at[0], halo_base + 3, (b, lax.min(z + 1, T - 1)))

    halo_part(0)
    pl.when(z > 0)(lambda: back_left().start())
    halo_part(1)
    pl.when(z < T - 1)(lambda: back_right().start())
    for i in range(T):
        s2_finish(0, i)

    def own_grad(r):
        g = nn(act[r], mat(Wq)) + nn(pairs[r, 1, :, pl.ds(0, depth)], mat(Wk))
        gin_ref[r] = g + nn(pairs[r, 1, :, pl.ds(depth, depth)], mat(Wv))

    loop(rows, own_grad)
    x_again.start()
    f2_finish(1)
    f2_finish(2)
    p3().wait()
    GP[y, x, c] = GP[y, x, c] + RP[1, 0, 1]
    for k in range(3, bits):
        cp = rc(GP.at[y, x, c], UPP.at[k - 3], up_base + k - 3, flip(k))
        cp.start()
        cp.wait()
        GP[y, x, c] = GP[y, x, c] + UPP[k - 3]
    FP[z, y, x, c] = GP[y, x, c]
    for i in others:
        pz(i).start()
    for i in range(T):
        s3_finish(0, i)

    pl.when(z > 0)(lambda: back_left().wait_send())
    pl.when(z < T - 1)(lambda: back_right().wait_send())
    pl.when(z < T - 1)(lambda: back_left().wait_recv())
    pl.when(z > 0)(lambda: back_right().wait_recv())
    x_again.wait()

    def norm_one_back(r, carry):
        xhat, rstd = norm_parts(act[r].astype(F32))
        grad = gin_ref[r] + hr[0, r].astype(F32) + hr[1, r].astype(F32)
        carry = carry + jnp.sum(grad * xhat, axis=0, keepdims=True)
        g = grad * gain1
        back = g - jnp.mean(g, axis=-1, keepdims=True) - xhat * jnp.mean(g * xhat, axis=-1, keepdims=True)
        gin_ref[r] = mid[r] + rstd * back
        return carry

    gain1_grad = lax.fori_loop(0, rows, norm_one_back, jnp.zeros((1, depth), F32))

    g_base = take(bits + T)
    GA[0] = jnp.where(row_of == 0, gain1_grad, gain2_grad)

    def ga(k):
        return rc(GA.at[k], GR.at[k], g_base + k, flip(k))

    def gz(i):
        return rc(GA.at[bits], GR.at[bits + z], g_base + bits + i, (b, slab(i)))

    def gains_step(k):
        ga(k).wait()
        GA[k + 1] = GA[k] + GR[k]
        if k + 1 < bits:
            ga(k + 1).start()
        else:
            GR[bits + z] = GA[bits]
            for i in others:
                gz(i).start()

    ga(0).start()
    f3_finish(1)
    f3_finish(2)
    gains_step(0)
    for i in others:
        pz(i).wait()
    pa1().start()
    gains_step(1)
    z_finish(0)
    gains_step(2)
    for k in range(3, bits):
        gains_step(k)
    pa1().wait()
    pa2().start()
    f1_finish(0)
    for i in others:
        gz(i).wait()
    total = GR[bits]
    for i in range(1, T):
        total = total + GR[bits + i]
    gains_ref[...] = total
    pa2().wait()
    pa3().start()
    f2_finish(0)
    pa3().wait()
    fp_copy = pltpu.make_async_copy(FP, fp_out, lsem.at[3])
    fp_copy.start()
    f3_finish(0)
    for g in range(3):
        for k in range(2):
            out_copy(g, k).wait()
    fp_copy.wait()


def per_device(
    tiles,
    batch,
    inputs,
    lengths,
    gain_one,
    qkv_weight,
    out_weight,
    gain_two,
    up_projection_weight,
    down_projection_weight,
    pair_bias,
    cotangent,
):
    tile, rows, depth = inputs.shape
    bits = batch.bit_length() - 1
    channels = qkv_weight.shape[2]
    piece = depth // 8
    window = pair_bias.shape[1]
    strip = tile // 8
    x = jnp.transpose(inputs, (1, 0, 2))
    cot = jnp.transpose(cotangent, (1, 0, 2))
    cut = (2, 2, 2, piece, depth)
    w0 = jnp.concatenate([jnp.transpose(qkv_weight, (0, 2, 1)), out_weight[None]]).reshape(cut)
    w1 = up_projection_weight.reshape(cut)
    w2 = down_projection_weight.reshape(cut)
    n_sems = 256 if bits == 3 else 288
    tokens = (rows, tile, depth)
    T = tiles
    vmem = pl.BlockSpec(memory_space=pltpu.VMEM)
    hbm = pl.BlockSpec(memory_space=pl.ANY)
    blocks = (T, 2, 2, 2, piece, depth)
    upper = max(bits - 3, 1)
    scratch = [
        pltpu.VMEM((2, 2, T, 2, piece, depth), BF),
        pltpu.VMEM(blocks, BF),
        pltpu.VMEM(blocks, BF),
        pltpu.VMEM(blocks, BF),
        pltpu.VMEM(blocks, BF),
        pltpu.VMEM(blocks, BF),
        pltpu.VMEM(blocks, BF),
        pltpu.VMEM((rows, 3, tile, depth), BF),
        pltpu.VMEM((rows, 3, tile, 2 * depth), BF),
        pltpu.VMEM(tokens, F32),
        pltpu.VMEM(tokens, F32),
        pltpu.VMEM(tokens, F32),
        pltpu.VMEM(tokens, F32),
        pltpu.VMEM(tokens, BF),
        pltpu.VMEM(tokens, BF),
        pltpu.VMEM(tokens, BF),
        pltpu.VMEM((rows, tile, 2 * depth), BF),
        pltpu.VMEM(tokens, F32),
        pltpu.VMEM((2,) + tokens, BF),
        pltpu.VMEM((tile, 3 * tile), BF),
        pltpu.VMEM((2, 2, 2, strip, window), BF),
        pltpu.VMEM((2, 2, 2, strip, window), BF),
        pltpu.VMEM((T, 2, 2, 2, strip, window), BF),
        pltpu.VMEM((2, 8, 2 * depth), F32),
        pltpu.VMEM((2, T - 1, 8, 2 * depth), F32),
        pltpu.VMEM((2, 8, 2 * depth), F32),
        pltpu.VMEM((bits + 1, 8, depth), F32),
        pltpu.VMEM((bits + T, 8, depth), F32),
        pltpu.VMEM((upper, strip, window), BF),
        pltpu.SemaphoreType.DMA((n_sems,)),
        pltpu.SemaphoreType.DMA((n_sems,)),
        pltpu.SemaphoreType.DMA((11,)),
        pltpu.SemaphoreType.REGULAR,
        pltpu.SemaphoreType.REGULAR((3, upper)),
    ]
    mixed, grad_inputs, gains, sums, pair = pl.pallas_call(
        functools.partial(kernel, T, bits, T * tile, n_sems),
        out_shape=(
            jax.ShapeDtypeStruct(tokens, BF),
            jax.ShapeDtypeStruct(tokens, F32),
            jax.ShapeDtypeStruct((8, depth), F32),
            jax.ShapeDtypeStruct((3,) + cut, BF),
            jax.ShapeDtypeStruct((T, 2, 2, 2, strip, window), BF),
        ),
        in_specs=[pl.BlockSpec(memory_space=pltpu.SMEM), hbm, vmem, vmem, vmem, hbm, hbm, hbm, hbm],
        out_specs=(vmem, vmem, vmem, hbm, hbm),
        scratch_shapes=scratch,
        compiler_params=pltpu.CompilerParams(
            collective_id=0, has_side_effects=True, vmem_limit_bytes=VMEM_BYTES
        ),
    )(
        lengths,
        x,
        cot,
        gain_one.astype(F32)[None],
        gain_two.astype(F32)[None],
        w0,
        w1,
        w2,
        pair_bias,
    )
    sums = sums.reshape(3, depth, depth).astype(F32)
    first = sums[0].reshape(4, channels, depth)
    return (
        jnp.transpose(mixed, (1, 0, 2)),
        jnp.transpose(grad_inputs, (1, 0, 2)),
        gains[0],
        jnp.transpose(first[:3], (0, 2, 1)),
        first[3],
        gains[1],
        sums[1],
        sums[2],
        pair.reshape(T * tile, window).astype(F32),
    )


def solution(mesh):
    return jax.shard_map(
        functools.partial(per_device, mesh.shape["tensor"], mesh.shape["batch"]),
        mesh=mesh,
        in_specs=(
            P("tensor", "batch", None),
            P("batch"),
            P(),
            P(None, None, "tensor"),
            P("tensor", None),
            P(),
            P(None, "tensor"),
            P("tensor", None),
            P(),
            P("tensor", "batch", None),
        ),
        out_specs=(
            P("tensor", "batch", None),
            P("tensor", "batch", None),
            P(),
            P(None, None, "tensor"),
            P("tensor", None),
            P(),
            P(None, "tensor"),
            P("tensor", None),
            P(),
        ),
        check_vma=False,
    )
```

```python
import functools

import jax
import jax.numpy as jnp
from jax import lax
from jax.experimental import pallas as pl
from jax.experimental.pallas import tpu as pltpu
from jax.sharding import PartitionSpec as P

MESH = pl.DeviceIdType.MESH
BF = jnp.bfloat16
F32 = jnp.float32
GELU_A = 0.044715
GELU_C = 0.7978845608028654
VMEM_BYTES = 63 << 20


def dot(a, b, ca, cb):
    return lax.dot_general(a, b, (((ca,), (cb,)), ((), ())), preferred_element_type=F32)


def nn(a, b):
    return dot(a, b, 1, 0)


def nt(a, b):
    return dot(a, b, 1, 1)


def tn(a, b):
    return dot(a, b, 0, 0)


def norm_parts(v):
    shifted = v - jnp.mean(v, axis=-1, keepdims=True)
    rstd = lax.rsqrt(jnp.mean(shifted * shifted, axis=-1, keepdims=True) + 1e-05)
    return shifted * rstd, rstd


def kernel(
    tiles,
    bits,
    length,
    n_sems,
    len_ref,
    x_ref,
    cot_ref,
    gain1_ref,
    gain2_ref,
    w0_in,
    w1_in,
    w2_in,
    bias_in,
    mixed_ref,
    gin_ref,
    gains_ref,
    f_out,
    fp_out,
    W0,
    W1,
    W2,
    G1,
    G2,
    R1,
    R2,
    n1,
    pairs,
    gates,
    ratio,
    dinv,
    mid,
    act,
    n2,
    mix,
    gs,
    gn2,
    hr,
    band,
    GP,
    RP,
    FP,
    CS,
    CSR,
    far,
    GA,
    GR,
    UPP,
    ssem,
    rsem,
    lsem,
    ready,
    upper_ready,
):
    T = tiles
    rows, tile, depth = cot_ref.shape
    piece = W1.shape[4]
    half = piece // 2
    b = lax.axis_index("batch")
    z = lax.axis_index("tensor")
    c = lax.rem(b, 2)
    x = lax.rem(b // 2, 2)
    y = lax.rem(b // 4, 2)
    gh = mixed_ref

    def flip(k):
        q = lax.rem(b // (1 << k), 2)
        return (b + (1 << k) - 2 * (1 << k) * q, z)

    core, xp, yp = flip(0), flip(1), flip(2)
    counter = [0]

    def take(n):
        counter[0] += n
        assert counter[0] <= n_sems
        return counter[0] - n

    def rc(src, dst, sem, dev, sent=None):
        return pltpu.make_async_remote_copy(
            src_ref=src,
            dst_ref=dst,
            send_sem=ssem.at[sem if sent is None else sent],
            recv_sem=rsem.at[sem],
            device_id=dev,
            device_id_type=MESH,
        )

    def slab(i):
        return lax.rem(z + i, T)

    def nth(k):
        near = [sorted(range(T), key=lambda j: (abs(j - q), j))[k] for q in range(T)]
        return sum(near[q] * (1 - lax.min(lax.abs(z - q), 1)) for q in range(T))

    slabs = [z] + [nth(k) for k in range(1, T)]
    lo, hi = pl.ds(0, half), pl.ds(half, half)
    partners = [flip(k) for k in range(bits)] + [(b, slab(i)) for i in range(1, T)]

    def w_at(g, j):
        return W0.at[:, :, j] if g == 0 else (W1, W2)[g - 1].at[j]

    w_in = (w0_in, w1_in, w2_in)
    local = [pltpu.make_async_copy(w_in[g], w_at(g, z), lsem.at[g]) for g in range(3)]
    window = bias_in.shape[1]
    bias = gn2.at[0, :, pl.ds(0, window)]
    local.append(pltpu.make_async_copy(bias_in.at[pl.ds(z * tile, tile)], bias, lsem.at[3]))
    local.append(pltpu.make_async_copy(x_ref, n1.at[:, 1], lsem.at[4]))
    for cp in local:
        cp.start()

    barrier = pltpu.get_barrier_semaphore()
    for dev in partners:
        pl.semaphore_signal(barrier, inc=1, device_id=dev, device_id_type=MESH)
    pl.semaphore_wait(barrier, len(partners))

    z_base, a1_base, a2_base, a3_base = take(3 * T), take(6 * T), take(6 * T), take(3 * T)
    own_base = take(6)
    right, left = (b, lax.min(z + 1, T - 1)), (b, lax.max(z - 1, 0))
    has_right, has_left = z < T - 1, z > 0

    def piece_at(g, j):
        return W0.at[y, x, j, c] if g == 0 else (W1, W2)[g - 1].at[j, y, x, c]

    def own_send(g, side):
        dst = piece_at(g, z)
        return rc(w_in[g].at[y, x, c], dst, z_base + g * T + z, (right, left)[side], own_base + 2 * g + side)

    def pass_on(g, k, side):
        ref = piece_at(g, slabs[k])
        return rc(ref, ref, z_base + g * T + slabs[k], (right, left)[side])

    def ag_1(g, k, h):
        ref = piece_at(g, slabs[k]).at[(lo, hi)[h]]
        return rc(ref, ref, a1_base + (g * 2 + h) * T + k, (xp, yp)[h])

    def ag_2(g, k, h):
        j = slabs[k]
        W = (W0, W1, W2)[g]
        if h == 0:
            ref = W.at[y, :, j, c, lo] if g == 0 else W.at[j, y, :, c, lo]
        else:
            ref = W.at[:, x, j, c, hi] if g == 0 else W.at[j, :, x, c, hi]
        return rc(ref, ref, a2_base + (g * 2 + h) * T + k, (yp, xp)[h])

    def ag_3(g, k):
        j = slabs[k]
        ref = W0.at[:, :, j, c] if g == 0 else (W1, W2)[g - 1].at[j, :, :, c]
        return rc(ref, ref, a3_base + g * T + k, core)

    others = range(1, T)

    def z_start(*groups):
        for side, there in ((0, has_right), (1, has_left)):

            @pl.when(there)
            def _():
                for g in groups:
                    own_send(g, side).start()

    def passing(k):
        j = slabs[k]
        return ((0, (j < z) & has_right), (1, (j > z) & has_left))

    def to_1(k, *groups):
        for g in groups:
            pass_on(g, k, 0).wait_recv()
            for side, there in passing(k):
                pl.when(there)(lambda: pass_on(g, k, side).start())
            for h in range(2):
                ag_1(g, k, h).start()

    def to_2(k, *groups):
        for g in groups:
            for h in range(2):
                ag_1(g, k, h).wait()
                ag_2(g, k, h).start()

    def to_3(k, *groups):
        for g in groups:
            for h in range(2):
                ag_2(g, k, h).wait()
            ag_3(g, k).start()

    def arrived(k, *groups):
        for g in groups:
            ag_3(g, k).wait()
            for side, there in passing(k):
                pl.when(there)(lambda: pass_on(g, k, side).wait_send())

    def z_sent(*groups):
        for side, there in ((0, has_right), (1, has_left)):

            @pl.when(there)
            def _():
                for g in groups:
                    own_send(g, side).wait_send()

    halo_base = take(2 * rows + 2)

    def halo_right(r):
        return rc(x_ref.at[r], n1.at[r, 0], halo_base + 2 + 2 * r, right)

    def halo_left(r):
        return rc(x_ref.at[r], n1.at[r, 2], halo_base + 3 + 2 * r, left)

    z_start(0)

    @pl.when(z == 0)
    def _():
        n1[:, 0] = jnp.zeros((rows, tile, depth), BF)
        hr[0] = jnp.zeros((rows, tile, depth), BF)

    @pl.when(z == T - 1)
    def _():
        n1[:, 2] = jnp.zeros((rows, tile, depth), BF)
        hr[1] = jnp.zeros((rows, tile, depth), BF)

    gain1 = gain1_ref[...]
    gain2 = gain2_ref[...]

    def loop(n, body):
        def step(i, carry):
            body(i)
            return carry

        lax.fori_loop(0, n, step, 0)

    def norm_tile(r, t):
        xhat, _ = norm_parts(n1[r, t].astype(F32))
        n1[r, t] = (xhat * gain1).astype(BF)

    local[3].wait()
    wide = jnp.concatenate([jnp.exp(bias[...]), jnp.ones((tile, 3 * tile - window), F32)], axis=1)
    band[...] = pltpu.roll(wide, 0, 1, stride=1, stride_axis=0).astype(BF)
    local[4].wait()
    loop(rows, lambda r: norm_tile(r, 1))

    def mat(ref):
        return ref[...].reshape(depth, depth)

    Wq, Wk, Wv, Wo = W0.at[0, 0], W0.at[0, 1], W0.at[1, 0], W0.at[1, 1]

    to_1(1, 0)
    to_1(2, 0)

    def halo_start():
        for r in range(rows):
            pl.when(has_right)(lambda: halo_right(r).start())
            pl.when(has_left)(lambda: halo_left(r).start())

    to_2(1, 0)
    to_1(3, 0)
    halo_start()
    z_start(1, 2)
    to_2(2, 0)
    to_3(1, 0)
    to_2(3, 0)
    to_3(2, 0)
    to_3(3, 0)
    for k in others:
        arrived(k, 0)
    local[0].wait()

    def key_values(r, t):
        n = n1[r, t]
        pos = (z - 1 + t) * tile + lax.broadcasted_iota(jnp.int32, (tile, 1), 0)
        keep = (pos >= 0) & (pos < length) & (pos < len_ref[r])
        e = jnp.where(keep, jnp.exp(nt(n, mat(Wk))), 0.0)
        v = nt(n, mat(Wv))
        pairs[r, t, :, pl.ds(0, depth)] = (e * v).astype(BF)
        pairs[r, t, :, pl.ds(depth, depth)] = e.astype(BF)

    def own_qkv(r):
        gates[r] = jax.nn.sigmoid(nt(n1[r, 1], mat(Wq)))
        key_values(r, 1)

    loop(rows, own_qkv)

    ones = jnp.ones((8, tile), BF)
    row_of = lax.broadcasted_iota(jnp.int32, (8, 1), 0)
    cs_base = take(2 * T)

    def cs_send(k, i):
        return rc(CS.at[k], CSR.at[k, i - 1], cs_base + k * T + i, (b, slab(i)))

    def cs_start(k, first, second):
        CS[k] = jnp.where(row_of == 0, first, second)
        for i in others:
            cs_send(k, i).start()

    def cs_finish(k):
        total = jnp.zeros(far.shape[1:], F32)
        for i in others:
            cs_send(k, i).wait()
            distance = lax.abs(lax.rem(z - i + T, T) - z)
            total = total + jnp.where(distance >= 2, CSR[k, i - 1], 0.0)
        far[k] = total

    cs_start(0, nn(ones, pairs[0, 1]), nn(ones, pairs[1, 1]))

    def halo_kv(r):
        @pl.when(z > 0)
        def _():
            halo_left(r).wait_send()
            halo_right(r).wait_recv()

        @pl.when(z < T - 1)
        def _():
            halo_right(r).wait_send()
            halo_left(r).wait_recv()

        for t in (0, 2):
            norm_tile(r, t)
            key_values(r, t)

    loop(rows, halo_kv)
    to_1(1, 1, 2)
    cs_finish(0)

    x_again = pltpu.make_async_copy(x_ref, act, lsem.at[4])
    x_again.start()

    def mixer(r):
        denom = nn(band[...], pairs[r, :, :, pl.ds(depth, depth)].reshape(3 * tile, depth))
        denom = denom + far[0, pl.ds(r, 1), pl.ds(depth, depth)]
        di = 1.0 / denom
        dinv[r] = di
        numer = nn(band[...], pairs[r, :, :, pl.ds(0, depth)].reshape(3 * tile, depth))
        rt = (numer + far[0, pl.ds(r, 1), pl.ds(0, depth)]) * di
        ratio[r] = rt
        mix[r] = (gates[r] * rt).astype(BF)

    mixer(0)
    to_1(2, 1, 2)
    mixer(1)
    to_2(1, 1, 2)
    x_again.wait()

    def middle(r):
        m = act[r].astype(F32) + nn(mix[r], mat(Wo))
        mid[r] = m
        gin_ref[r] = m
        xhat, _ = norm_parts(m)
        n2[r] = (xhat * gain2).astype(BF)
        gn2[r] = jnp.zeros((tile, depth), F32)

    loop(rows, middle)
    local[1].wait()
    local[2].wait()

    G = (W1, G1, G2)
    R = (W2, R1, R2)
    s1_base, s2_base, s3_base, sz_base, f_base = take(12), take(24), take(24), take(3 * T), take(15)
    def s1(g, o):
        j = slabs[o]
        return rc(G[g].at[j, :, :, 1 - c], R[g].at[j, :, :, 0], s1_base + g * 4 + o, core)

    def s1_kind(ty, tx):
        return rc(G[0].at[:, ty, tx, 1 - c], R[0].at[:, ty, tx, 0], s1_base + 2 * ty + tx, core)

    def s2(g, o, h):
        j = slabs[o]
        if h == 0:
            src, dst, dev = G[g].at[j, :, 1 - x, c, lo], R[g].at[j, 0, :, 1, lo], xp
        else:
            src, dst, dev = G[g].at[j, 1 - y, :, c, hi], R[g].at[j, 0, :, 1, hi], yp
        return rc(src, dst, s2_base + (g * 2 + h) * 4 + o, dev)

    def s2_kind(late, h):
        if h == 0:
            k = x if late else 1 - x
            src, dst, dev = G[0].at[:, k, 1 - x, c, lo], R[0].at[:, 0, k, 1, lo], xp
        else:
            k = y if late else 1 - y
            src, dst, dev = G[0].at[:, 1 - y, k, c, hi], R[0].at[:, 0, k, 1, hi], yp
        return rc(src, dst, s2_base + h * 4 + late, dev)

    def s3(g, o, h):
        j = slabs[o]
        if h == 0:
            src, dst, dev = G[g].at[j, 1 - y, x, c, lo], R[g].at[j, 1, 0, 1, lo], yp
        else:
            src, dst, dev = G[g].at[j, y, 1 - x, c, hi], R[g].at[j, 1, 0, 1, hi], xp
        return rc(src, dst, s3_base + (g * 2 + h) * 4 + o, dev)

    def sz(g, o):
        j = lax.rem(z - o + T, T)
        return rc(G[g].at[j, y, x, c], R[g].at[o - 1, 1, 1, 1], sz_base + g * T + o, (b, j))

    def sz_slab(g, k):
        j = slabs[k]
        o = lax.rem(z - j + T, T)
        return rc(G[g].at[j, y, x, c], R[g].at[o - 1, 1, 1, 1], sz_base + g * T + o, (b, j))

    def s1_finish(o, *groups):
        j = slabs[o]
        for g in groups:
            s1(g, o).wait()
            G[g][j, :, :, c] = G[g][j, :, :, c] + R[g][j, :, :, 0]
            for h in range(2):
                s2(g, o, h).start()

    def s1_kind_finish(ty, tx):
        s1_kind(ty, tx).wait()
        G[0][:, ty, tx, c] = G[0][:, ty, tx, c] + R[0][:, ty, tx, 0]

    def s2_finish(o, *groups):
        j = slabs[o]
        for g in groups:
            s2(g, o, 0).wait()
            G[g][j, :, x, c, lo] = G[g][j, :, x, c, lo] + R[g][j, 0, :, 1, lo]
            s3(g, o, 0).start()
            s2(g, o, 1).wait()
            G[g][j, y, :, c, hi] = G[g][j, y, :, c, hi] + R[g][j, 0, :, 1, hi]
            s3(g, o, 1).start()

    def s2_kind_finish(late):
        for h in range(2):
            s2_kind(late, h).wait()
        k = 1 - x if late else x
        G[0][:, k, x, c, lo] = G[0][:, k, x, c, lo] + R[0][:, 0, k, 1, lo]
        k = 1 - y if late else y
        G[0][:, y, k, c, hi] = G[0][:, y, k, c, hi] + R[0][:, 0, k, 1, hi]

    def s3_finish(o, *groups):
        j = slabs[o]
        for g in groups:
            s3(g, o, 0).wait()
            s3(g, o, 1).wait()
            G[g][j, y, x, c] = G[g][j, y, x, c] + R[g][j, 1, 0, 1]
            if o:
                sz_slab(g, o).start()

    def f_at(g):
        return G[g].at[:, :, :, 1 - c]

    def f1(g, h):
        rng = (lo, hi)[h]
        other = f_at(g).at[c, y, x, rng]
        return rc(other, other, f_base + 5 * g + h, (xp, yp)[h])

    def f2(g, h):
        ref = f_at(g).at[c, y, :, lo] if h == 0 else f_at(g).at[c, :, x, hi]
        return rc(ref, ref, f_base + 5 * g + 2 + h, (yp, xp)[h])

    def f3(g):
        return rc(f_at(g).at[c], G[g].at[c, :, :, c], f_base + 5 * g + 4, core)

    u_base = take(4 * max(bits - 3, 0))

    def z_finish(g):
        total = G[g][z, y, x, c].astype(F32)
        for o in others:
            sz(g, o).wait()
            total = total + R[g][o - 1, 1, 1, 1].astype(F32)
        mine = f_at(g).at[c, y, x]
        mine[...] = total.astype(BF)
        for k in range(3, bits):
            u = k - 3
            slot = f_at(g).at[2 + u // 4, u // 2 % 2, u % 2]
            pl.semaphore_signal(upper_ready.at[g, u], inc=1, device_id=flip(k), device_id_type=MESH)
            pl.semaphore_wait(upper_ready.at[g, u], 1)
            cp = rc(mine, slot, u_base + g * (bits - 3) + u, flip(k))
            cp.start()
            cp.wait()
            mine[...] = mine[...] + slot[...]
        for h in range(2):
            f1(g, h).start()

    def f1_finish(g):
        for h in range(2):
            f1(g, h).wait()
            f2(g, h).start()

    def f2_finish(g):
        for h in range(2):
            f2(g, h).wait()
        f3(g).start()

    def out_copy(g, k):
        src = G[g].at[k, :, :, 1 - c]
        return pltpu.make_async_copy(src, f_out.at[g, :, :, k], lsem.at[5 + 2 * g + k])

    def f3_finish(g):
        f3(g).wait()
        for k in range(2):
            out_copy(g, k).start()

    def feed(o, between, after_part, after_down):
        j = slabs[o]
        up, down = W1.at[j], W2.at[j]

        def part(r):
            for k in range(3):
                cols = pl.ds(k * (depth // 3), depth // 3)
                h = nn(n2[r], up[:, :, :, :, cols].reshape(depth, depth // 3))
                ga = nt(cot_ref[r], down[...].reshape(depth, depth)[k * (depth // 3) : (k + 1) * (depth // 3)])
                sq = h * h
                t = jnp.tanh(GELU_C * h * (1.0 + GELU_A * sq))
                hh = 0.5 * h
                act[r, :, cols] = (hh + hh * t).astype(BF)
                slope = 0.5 + 0.5 * t + hh * (1.0 - t * t) * (GELU_C + (3.0 * GELU_C * GELU_A) * sq)
                gh[r, :, cols] = (ga * slope).astype(BF)
            gin_ref[r] += nn(act[r], mat(down))
            gn2[r] += nt(gh[r], mat(up))
            pl.when(r == 0)(between)

        loop(rows, part)
        after_part()
        for m in range(2):
            cols = pl.ds(m * (depth // 2), depth // 2)
            d = tn(act[:, :, cols].reshape(rows * tile, depth // 2), cot_ref[...].reshape(rows * tile, depth))
            G2[j, m] = d.astype(BF).reshape(2, 2, piece, depth)
        s1(2, o).start()
        after_down()
        for m in range(2):
            cols = pl.ds(m * (depth // 2), depth // 2)
            d = tn(n2[:, :, cols].reshape(rows * tile, depth // 2), gh[...].reshape(rows * tile, depth))
            G1[j, m] = d.astype(BF).reshape(2, 2, piece, depth)
        s1(1, o).start()

    def nothing():
        return

    def own_between():
        to_2(2, 1, 2)
        to_3(1, 1, 2)

    def own_part():
        to_1(3, 1, 2)
        to_3(2, 1, 2)

    def own_down():
        to_2(3, 1, 2)

    feed(0, own_between, own_part, own_down)
    arrived(1, 1, 2)

    def second_between():
        s1_finish(0, 2, 1)

    def second_part():
        to_3(3, 1, 2)

    feed(1, second_between, second_part, nothing)
    arrived(2, 1, 2)

    def third_between():
        s1_finish(1, 2, 1)

    def third_part():
        s2_finish(0, 2, 1)

    feed(2, third_between, third_part, nothing)
    arrived(3, 1, 2)
    z_sent(0, 1, 2)

    def fourth_between():
        s1_finish(2, 2, 1)

    def fourth_part():
        s2_finish(1, 2, 1)

    def fourth_down():
        s3_finish(0, 2, 1)

    feed(3, fourth_between, fourth_part, fourth_down)
    for dev in partners:
        pl.semaphore_signal(ready, inc=1, device_id=dev, device_id_type=MESH)

    def norm_two_back(r, carry):
        mixed_ref[r] = gin_ref[r].astype(BF)
        xhat, rstd = norm_parts(mid[r])
        grad = gn2[r]
        carry = carry + jnp.sum(grad * xhat, axis=0, keepdims=True)
        g = grad * gain2
        back = g - jnp.mean(g, axis=-1, keepdims=True) - xhat * jnp.mean(g * xhat, axis=-1, keepdims=True)
        gm = cot_ref[r].astype(F32) + rstd * back
        mid[r] = gm
        n2[r] = gm.astype(BF)
        return carry

    gain2_grad = lax.fori_loop(0, rows, norm_two_back, jnp.zeros((1, depth), F32))

    s1_finish(3, 2, 1)
    pl.semaphore_wait(ready, len(partners))

    local[3].start()

    def kind(ty, tx, lhs, start, rhs):
        for m in range(2):
            part = lhs[..., pl.ds(start + m * (depth // 2), depth // 2)]
            d = tn(part.reshape(rhs.shape[0], depth // 2), rhs).astype(BF)
            d = d.reshape(2, 2, piece, depth)
            for s in range(2):
                G[0][2 * m + s, ty, tx] = d[s]
        s1_kind(ty, tx).start()

    flat = (rows * tile, depth)
    kind(1, 1, mix, 0, n2[...].reshape(flat))
    s2_finish(2, 2, 1)

    def mixer_back(r):
        gmix = nt(n2[r], mat(Wo))
        gate = gates[r]
        rt = ratio[r]
        first = gmix * gate
        act[r] = (first * rt * (1.0 - gate)).astype(BF)
        first = first * dinv[r]
        gs[r, :, pl.ds(0, depth)] = first.astype(BF)
        gs[r, :, pl.ds(depth, depth)] = (-first * rt).astype(BF)

    loop(rows, mixer_back)
    cs_start(1, nn(ones, gs[0]), nn(ones, gs[1]))
    kind(0, 0, act, 0, n1[:, 1].reshape(flat))
    s3_finish(1, 2, 1)
    s1_kind_finish(1, 1)
    s1_kind_finish(0, 0)
    for h in range(2):
        s2_kind(0, h).start()

    local[3].wait()
    gband = nt(gs[0], pairs[0].reshape(3 * tile, 2 * depth)) + nt(gs[1], pairs[1].reshape(3 * tile, 2 * depth))
    shift = lax.broadcasted_iota(jnp.int32, (tile, 1), 0)
    k = 1
    while k < tile:
        gband = jnp.where(lax.rem(shift // k, 2) == 1, pltpu.roll(gband, 3 * tile - k, 1), gband)
        k *= 2
    gp = (gband[:, :window] * jnp.exp(bias[...])).astype(BF)
    GP[...] = gp.reshape(GP.shape)
    p_base = take(6 + T)
    up_base = u_base + 3 * max(bits - 3, 0)

    def p1():
        return rc(GP.at[:, :, 1 - c], RP.at[:, :, 0], p_base, core)

    def p2():
        return rc(GP.at[:, 1 - x, c], RP.at[0, :, 1], p_base + 1, xp)

    def p3():
        return rc(GP.at[1 - y, x, c], RP.at[1, 0, 1], p_base + 2, yp)

    def pz(i):
        mine = FP.at[z, y, x, c]
        return rc(mine, mine, p_base + 6 + i, (b, slab(i)))

    def pa1():
        ref = FP.at[:, y, x, c]
        return rc(ref, ref, p_base + 3, xp)

    def pa2():
        ref = FP.at[:, y, :, c]
        return rc(ref, ref, p_base + 4, yp)

    def pa3():
        ref = FP.at[:, :, :, c]
        return rc(ref, ref, p_base + 5, core)

    p1().start()
    s2_finish(3, 2, 1)
    cs_finish(1)

    def pairs_back(r):
        for t in range(3):
            near = band[:, pl.ds(t * tile, tile)]
            gn = tn(near, gs[r, :, pl.ds(0, depth)])
            gd = tn(near, gs[r, :, pl.ds(depth, depth)])
            if t == 1:
                gn = gn + far[1, pl.ds(r, 1), pl.ds(0, depth)]
                gd = gd + far[1, pl.ds(r, 1), pl.ds(depth, depth)]
            wv = pairs[r, t, :, pl.ds(0, depth)].astype(F32)
            we = pairs[r, t, :, pl.ds(depth, depth)].astype(F32)
            pairs[r, t, :, pl.ds(0, depth)] = (gn * wv + gd * we).astype(BF)
            pairs[r, t, :, pl.ds(depth, depth)] = (gn * we).astype(BF)

    pairs_back(0)
    s3_finish(2, 2, 1)
    pairs_back(1)
    p1().wait()
    GP[:, :, c] = GP[:, :, c] + RP[:, :, 0]
    p2().start()
    n1_all = n1[...].reshape(3 * rows * tile, depth)
    kind(0, 1, pairs, 0, n1_all)
    s3_finish(3, 2, 1)
    kind(1, 0, pairs, depth, n1_all)
    s1_kind_finish(0, 1)
    s1_kind_finish(1, 0)
    for h in range(2):
        s2_kind(1, h).start()
    p2().wait()
    GP[:, x, c] = GP[:, x, c] + RP[0, :, 1]
    p3().start()

    def halo_part(d):
        def body(r):
            g = nn(pairs[r, 2 * d, :, pl.ds(0, depth)], mat(Wk))
            g = g + nn(pairs[r, 2 * d, :, pl.ds(depth, depth)], mat(Wv))
            gs[r, :, pl.ds(d * depth, depth)] = g.astype(BF)

        loop(rows, body)

    def back_left():
        return rc(gs.at[:, :, pl.ds(0, depth)], hr.at[1], halo_base, left)

    def back_right():
        return rc(gs.at[:, :, pl.ds(depth, depth)], hr.at[0], halo_base + 1, right)

    halo_part(0)
    pl.when(z > 0)(lambda: back_left().start())
    halo_part(1)
    pl.when(z < T - 1)(lambda: back_right().start())
    s2_kind_finish(0)
    s2_kind_finish(1)
    for o in (1, 2, 3, 0):
        for h in range(2):
            s3(0, o, h).start()
    z_finish(2)
    z_finish(1)

    def own_grad(r):
        g = nn(act[r], mat(Wq)) + nn(pairs[r, 1, :, pl.ds(0, depth)], mat(Wk))
        gin_ref[r] = g + nn(pairs[r, 1, :, pl.ds(depth, depth)], mat(Wv))

    loop(rows, own_grad)
    x_again.start()
    f1_finish(2)
    f1_finish(1)
    p3().wait()
    GP[y, x, c] = GP[y, x, c] + RP[1, 0, 1]
    for k in range(3, bits):
        cp = rc(GP.at[y, x, c], UPP.at[k - 3], up_base + k - 3, flip(k))
        cp.start()
        cp.wait()
        GP[y, x, c] = GP[y, x, c] + UPP[k - 3]
    FP[z, y, x, c] = GP[y, x, c]
    for i in others:
        pz(i).start()
    for o in (1, 2, 3, 0):
        s3_finish(o, 0)
    f2_finish(2)
    f2_finish(1)

    pl.when(z > 0)(lambda: back_left().wait_send())
    pl.when(z < T - 1)(lambda: back_right().wait_send())
    pl.when(z < T - 1)(lambda: back_left().wait_recv())
    pl.when(z > 0)(lambda: back_right().wait_recv())
    x_again.wait()

    def norm_one_back(r, carry):
        xhat, rstd = norm_parts(act[r].astype(F32))
        grad = gin_ref[r] + hr[0, r].astype(F32) + hr[1, r].astype(F32)
        carry = carry + jnp.sum(grad * xhat, axis=0, keepdims=True)
        g = grad * gain1
        back = g - jnp.mean(g, axis=-1, keepdims=True) - xhat * jnp.mean(g * xhat, axis=-1, keepdims=True)
        gin_ref[r] = mid[r] + rstd * back
        return carry

    gain1_grad = lax.fori_loop(0, rows, norm_one_back, jnp.zeros((1, depth), F32))

    g_base = take(bits + T)
    GA[0] = jnp.where(row_of == 0, gain1_grad, gain2_grad)

    def ga(k):
        return rc(GA.at[k], GR.at[k], g_base + k, flip(k))

    def gz(i):
        return rc(GA.at[bits], GR.at[bits + z], g_base + bits + i, (b, slab(i)))

    def gains_step(k):
        ga(k).wait()
        GA[k + 1] = GA[k] + GR[k]
        if k + 1 < bits:
            ga(k + 1).start()
        else:
            GR[bits + z] = GA[bits]
            for i in others:
                gz(i).start()

    ga(0).start()
    f3_finish(1)
    f3_finish(2)
    gains_step(0)
    for i in others:
        pz(i).wait()
    pa1().start()
    gains_step(1)
    z_finish(0)
    gains_step(2)
    for k in range(3, bits):
        gains_step(k)
    pa1().wait()
    pa2().start()
    f1_finish(0)
    for i in others:
        gz(i).wait()
    total = GR[bits]
    for i in range(1, T):
        total = total + GR[bits + i]
    gains_ref[...] = total
    pa2().wait()
    pa3().start()
    f2_finish(0)
    pa3().wait()
    fp_copy = pltpu.make_async_copy(FP, fp_out, lsem.at[3])
    fp_copy.start()
    f3_finish(0)
    for g in range(3):
        for k in range(2):
            out_copy(g, k).wait()
    fp_copy.wait()


def per_device(
    tiles,
    batch,
    inputs,
    lengths,
    gain_one,
    qkv_weight,
    out_weight,
    gain_two,
    up_projection_weight,
    down_projection_weight,
    pair_bias,
    cotangent,
):
    tile, rows, depth = inputs.shape
    bits = batch.bit_length() - 1
    channels = qkv_weight.shape[2]
    piece = depth // 8
    window = pair_bias.shape[1]
    strip = tile // 8
    x = jnp.transpose(inputs, (1, 0, 2))
    cot = jnp.transpose(cotangent, (1, 0, 2))
    cut = (2, 2, 2, piece, depth)
    w0 = jnp.concatenate([jnp.transpose(qkv_weight, (0, 2, 1)), out_weight[None]]).reshape(cut)
    w1 = up_projection_weight.reshape(cut)
    w2 = down_projection_weight.reshape(cut)
    n_sems = 256 if bits == 3 else 288
    tokens = (rows, tile, depth)
    T = tiles
    vmem = pl.BlockSpec(memory_space=pltpu.VMEM)
    hbm = pl.BlockSpec(memory_space=pl.ANY)
    blocks = (T, 2, 2, 2, piece, depth)
    upper = max(bits - 3, 1)
    scratch = [
        pltpu.VMEM((2, 2, T, 2, piece, depth), BF),
        pltpu.VMEM(blocks, BF),
        pltpu.VMEM(blocks, BF),
        pltpu.VMEM(blocks, BF),
        pltpu.VMEM(blocks, BF),
        pltpu.VMEM(blocks, BF),
        pltpu.VMEM(blocks, BF),
        pltpu.VMEM((rows, 3, tile, depth), BF),
        pltpu.VMEM((rows, 3, tile, 2 * depth), BF),
        pltpu.VMEM(tokens, F32),
        pltpu.VMEM(tokens, F32),
        pltpu.VMEM(tokens, F32),
        pltpu.VMEM(tokens, F32),
        pltpu.VMEM(tokens, BF),
        pltpu.VMEM(tokens, BF),
        pltpu.VMEM(tokens, BF),
        pltpu.VMEM((rows, tile, 2 * depth), BF),
        pltpu.VMEM(tokens, F32),
        pltpu.VMEM((2,) + tokens, BF),
        pltpu.VMEM((tile, 3 * tile), BF),
        pltpu.VMEM((2, 2, 2, strip, window), BF),
        pltpu.VMEM((2, 2, 2, strip, window), BF),
        pltpu.VMEM((T, 2, 2, 2, strip, window), BF),
        pltpu.VMEM((2, 8, 2 * depth), F32),
        pltpu.VMEM((2, T - 1, 8, 2 * depth), F32),
        pltpu.VMEM((2, 8, 2 * depth), F32),
        pltpu.VMEM((bits + 1, 8, depth), F32),
        pltpu.VMEM((bits + T, 8, depth), F32),
        pltpu.VMEM((upper, strip, window), BF),
        pltpu.SemaphoreType.DMA((n_sems,)),
        pltpu.SemaphoreType.DMA((n_sems,)),
        pltpu.SemaphoreType.DMA((11,)),
        pltpu.SemaphoreType.REGULAR,
        pltpu.SemaphoreType.REGULAR((3, upper)),
    ]
    mixed, grad_inputs, gains, sums, pair = pl.pallas_call(
        functools.partial(kernel, T, bits, T * tile, n_sems),
        out_shape=(
            jax.ShapeDtypeStruct(tokens, BF),
            jax.ShapeDtypeStruct(tokens, F32),
            jax.ShapeDtypeStruct((8, depth), F32),
            jax.ShapeDtypeStruct((3,) + cut, BF),
            jax.ShapeDtypeStruct((T, 2, 2, 2, strip, window), BF),
        ),
        in_specs=[pl.BlockSpec(memory_space=pltpu.SMEM), hbm, vmem, vmem, vmem, hbm, hbm, hbm, hbm],
        out_specs=(vmem, vmem, vmem, hbm, hbm),
        scratch_shapes=scratch,
        compiler_params=pltpu.CompilerParams(
            collective_id=0, has_side_effects=True, vmem_limit_bytes=VMEM_BYTES
        ),
    )(
        lengths,
        x,
        cot,
        gain_one.astype(F32)[None],
        gain_two.astype(F32)[None],
        w0,
        w1,
        w2,
        pair_bias,
    )
    sums = sums.reshape(3, depth, depth).astype(F32)
    first = sums[0].reshape(4, channels, depth)
    return (
        jnp.transpose(mixed, (1, 0, 2)),
        jnp.transpose(grad_inputs, (1, 0, 2)),
        gains[0],
        jnp.transpose(first[:3], (0, 2, 1)),
        first[3],
        gains[1],
        sums[1],
        sums[2],
        pair.reshape(T * tile, window).astype(F32),
    )


def solution(mesh):
    return jax.shard_map(
        functools.partial(per_device, mesh.shape["tensor"], mesh.shape["batch"]),
        mesh=mesh,
        in_specs=(
            P("tensor", "batch", None),
            P("batch"),
            P(),
            P(None, None, "tensor"),
            P("tensor", None),
            P(),
            P(None, "tensor"),
            P("tensor", None),
            P(),
            P("tensor", "batch", None),
        ),
        out_specs=(
            P("tensor", "batch", None),
            P("tensor", "batch", None),
            P(),
            P(None, None, "tensor"),
            P("tensor", None),
            P(),
            P(None, "tensor"),
            P("tensor", None),
            P(),
        ),
        check_vma=False,
    )
```

```python
import functools

import jax
import jax.numpy as jnp
from jax import lax
from jax.experimental import pallas as pl
from jax.experimental.pallas import tpu as pltpu
from jax.sharding import PartitionSpec as P

MESH = pl.DeviceIdType.MESH
BF = jnp.bfloat16
F32 = jnp.float32
GELU_A = 0.044715
GELU_C = 0.7978845608028654
VMEM_BYTES = 63 << 20


def dot(a, b, ca, cb):
    return lax.dot_general(a, b, (((ca,), (cb,)), ((), ())), preferred_element_type=F32)


def nn(a, b):
    return dot(a, b, 1, 0)


def nt(a, b):
    return dot(a, b, 1, 1)


def tn(a, b):
    return dot(a, b, 0, 0)


def norm_parts(v):
    shifted = v - jnp.mean(v, axis=-1, keepdims=True)
    rstd = lax.rsqrt(jnp.mean(shifted * shifted, axis=-1, keepdims=True) + 1e-05)
    return shifted * rstd, rstd


def kernel(
    tiles,
    bits,
    length,
    n_sems,
    len_ref,
    x_ref,
    cot_ref,
    gain_ref,
    w0_in,
    w1_in,
    w2_in,
    bias_in,
    mixed_ref,
    gin_ref,
    gains1_ref,
    gains2_ref,
    fq_out,
    fo_out,
    f1_out,
    f2_out,
    fp_out,
    W0,
    W1,
    W2,
    G1,
    G2,
    R1,
    R2,
    n1,
    pairs,
    gates,
    ratio,
    dinv,
    mid,
    act,
    n2,
    mix,
    gs,
    gn2,
    hr,
    band,
    GP,
    RP,
    FP,
    CS,
    CSR,
    far,
    GA,
    GR,
    UPP,
    ssem,
    rsem,
    lsem,
    ready,
    upper_ready,
):
    T = tiles
    rows, tile, depth = cot_ref.shape
    piece = W1.shape[4]
    half = piece // 2
    b = lax.axis_index("batch")
    z = lax.axis_index("tensor")
    c = lax.rem(b, 2)
    x = lax.rem(b // 2, 2)
    y = lax.rem(b // 4, 2)
    gh = mixed_ref

    def flip(k):
        q = lax.rem(b // (1 << k), 2)
        return (b + (1 << k) - 2 * (1 << k) * q, z)

    core, xp, yp = flip(0), flip(1), flip(2)
    counter = [0]

    def take(n):
        counter[0] += n
        assert counter[0] <= n_sems
        return counter[0] - n

    def rc(src, dst, sem, dev, sent=None):
        return pltpu.make_async_remote_copy(
            src_ref=src,
            dst_ref=dst,
            send_sem=ssem.at[sem if sent is None else sent],
            recv_sem=rsem.at[sem],
            device_id=dev,
            device_id_type=MESH,
        )

    def slab(i):
        return lax.rem(z + i, T)

    def nth(k):
        near = [sorted(range(T), key=lambda j: (abs(j - q), j))[k] for q in range(T)]
        return sum(near[q] * (1 - lax.min(lax.abs(z - q), 1)) for q in range(T))

    slabs = [z] + [nth(k) for k in range(1, T)]
    lo, hi = pl.ds(0, half), pl.ds(half, half)
    partners = [flip(k) for k in range(bits)] + [(b, slab(i)) for i in range(1, T)]

    def w_at(g, j):
        return W0.at[:, :, j] if g == 0 else (W1, W2)[g - 1].at[j]

    w_in = (w0_in, w1_in, w2_in)
    local = [pltpu.make_async_copy(w_in[g], w_at(g, z), lsem.at[g]) for g in range(3)]
    window = bias_in.shape[1]
    bias = gn2.at[0, :, pl.ds(0, window)]
    local.append(pltpu.make_async_copy(bias_in.at[pl.ds(z * tile, tile)], bias, lsem.at[3]))
    local.append(pltpu.make_async_copy(x_ref, n1.at[:, 1], lsem.at[4]))
    for cp in local:
        cp.start()

    barrier = pltpu.get_barrier_semaphore()
    for dev in partners:
        pl.semaphore_signal(barrier, inc=1, device_id=dev, device_id_type=MESH)
    pl.semaphore_wait(barrier, len(partners))

    z_base, a1_base, a2_base, a3_base = take(3 * T), take(6 * T), take(6 * T), take(3 * T)
    own_base = take(6)
    right, left = (b, lax.min(z + 1, T - 1)), (b, lax.max(z - 1, 0))
    has_right, has_left = z < T - 1, z > 0

    def piece_at(g, j):
        return W0.at[y, x, j, c] if g == 0 else (W1, W2)[g - 1].at[j, y, x, c]

    def own_send(g, side):
        dst = piece_at(g, z)
        return rc(w_in[g].at[y, x, c], dst, z_base + g * T + z, (right, left)[side], own_base + 2 * g + side)

    def pass_on(g, k, side):
        ref = piece_at(g, slabs[k])
        return rc(ref, ref, z_base + g * T + slabs[k], (right, left)[side])

    def ag_1(g, k, h):
        ref = piece_at(g, slabs[k]).at[(lo, hi)[h]]
        return rc(ref, ref, a1_base + (g * 2 + h) * T + k, (xp, yp)[h])

    def ag_2(g, k, h):
        j = slabs[k]
        W = (W0, W1, W2)[g]
        if h == 0:
            ref = W.at[y, :, j, c, lo] if g == 0 else W.at[j, y, :, c, lo]
        else:
            ref = W.at[:, x, j, c, hi] if g == 0 else W.at[j, :, x, c, hi]
        return rc(ref, ref, a2_base + (g * 2 + h) * T + k, (yp, xp)[h])

    def ag_3(g, k):
        j = slabs[k]
        ref = W0.at[:, :, j, c] if g == 0 else (W1, W2)[g - 1].at[j, :, :, c]
        return rc(ref, ref, a3_base + g * T + k, core)

    others = range(1, T)

    def z_start(*groups):
        for side, there in ((0, has_right), (1, has_left)):

            @pl.when(there)
            def _():
                for g in groups:
                    own_send(g, side).start()

    def passing(k):
        j = slabs[k]
        return ((0, (j < z) & has_right), (1, (j > z) & has_left))

    def to_1(k, *groups):
        for g in groups:
            pass_on(g, k, 0).wait_recv()
            for side, there in passing(k):
                pl.when(there)(lambda: pass_on(g, k, side).start())
            for h in range(2):
                ag_1(g, k, h).start()

    def to_2(k, *groups):
        for g in groups:
            for h in range(2):
                ag_1(g, k, h).wait()
                ag_2(g, k, h).start()

    def to_3(k, *groups):
        for g in groups:
            for h in range(2):
                ag_2(g, k, h).wait()
            ag_3(g, k).start()

    def arrived(k, *groups):
        for g in groups:
            ag_3(g, k).wait()
            for side, there in passing(k):
                pl.when(there)(lambda: pass_on(g, k, side).wait_send())

    def z_sent(*groups):
        for side, there in ((0, has_right), (1, has_left)):

            @pl.when(there)
            def _():
                for g in groups:
                    own_send(g, side).wait_send()

    halo_base = take(2 * rows + 2)

    def halo_right(r):
        return rc(x_ref.at[r], n1.at[r, 0], halo_base + 2 + 2 * r, right)

    def halo_left(r):
        return rc(x_ref.at[r], n1.at[r, 2], halo_base + 3 + 2 * r, left)

    z_start(0)

    @pl.when(z == 0)
    def _():
        n1[:, 0] = jnp.zeros((rows, tile, depth), BF)
        hr[0] = jnp.zeros((rows, tile, depth), BF)

    @pl.when(z == T - 1)
    def _():
        n1[:, 2] = jnp.zeros((rows, tile, depth), BF)
        hr[1] = jnp.zeros((rows, tile, depth), BF)

    gain1 = gain_ref[0:1]
    gain2 = gain_ref[1:2]

    def loop(n, body, between=None):
        def step(i, carry):
            body(i)
            if between is not None:
                pl.when(i == 0)(between)
            return carry

        lax.fori_loop(0, n, step, 0)

    def norm_tile(r, t):
        xhat, _ = norm_parts(n1[r, t].astype(F32))
        n1[r, t] = (xhat * gain1).astype(BF)

    local[3].wait()
    wide = jnp.concatenate([jnp.exp(bias[...]), jnp.ones((tile, 3 * tile - window), F32)], axis=1)
    band[...] = pltpu.roll(wide, 0, 1, stride=1, stride_axis=0).astype(BF)
    local[4].wait()
    loop(rows, lambda r: norm_tile(r, 1))

    def mat(ref):
        return ref[...].reshape(depth, depth)

    Wq, Wk, Wv, Wo = W0.at[0, 0], W0.at[0, 1], W0.at[1, 0], W0.at[1, 1]

    def halo_start():
        for r in range(rows):
            pl.when(has_right)(lambda: halo_right(r).start())
            pl.when(has_left)(lambda: halo_left(r).start())

    at_end = (z == 0) | (z == T - 1)

    inside = z * (T - 1 - z) > 0

    def ends(step, *args):
        pl.when(at_end)(lambda: step(*args))

    def middles(step, *args):
        pl.when(inside)(lambda: step(*args))

    @pl.when(at_end)
    def _():
        z_start(2, 1)
        halo_start()

    to_1(1, 0)
    to_1(2, 0)
    to_2(1, 0)
    to_1(3, 0)

    @pl.when(inside)
    def _():
        z_start(2, 1)
        halo_start()

    to_2(2, 0)
    to_3(1, 0)
    to_2(3, 0)
    to_3(2, 0)
    to_1(1, 2, 1)
    middles(to_1, 2, 2, 1)
    to_3(3, 0)
    for k in others:
        arrived(k, 0)
    local[0].wait()

    def key_values(r, t):
        n = n1[r, t]
        pos = (z - 1 + t) * tile + lax.broadcasted_iota(jnp.int32, (tile, 1), 0)
        keep = (pos >= 0) & (pos < length) & (pos < len_ref[r])
        e = jnp.where(keep, jnp.exp(nt(n, mat(Wk))), 0.0)
        v = nt(n, mat(Wv))
        pairs[r, t, :, pl.ds(0, depth)] = (e * v).astype(BF)
        pairs[r, t, :, pl.ds(depth, depth)] = e.astype(BF)

    def own_qkv(r):
        gates[r] = jax.nn.sigmoid(nt(n1[r, 1], mat(Wq)))
        key_values(r, 1)

    loop(rows, own_qkv, lambda: to_2(1, 2, 1))
    middles(to_2, 2, 2, 1)

    ones = jnp.ones((8, tile), BF)
    row_of = lax.broadcasted_iota(jnp.int32, (8, 1), 0)
    cs_base = take(2 * T)

    def cs_send(k, i):
        return rc(CS.at[k], CSR.at[k, i - 1], cs_base + k * T + i, (b, slab(i)))

    def cs_start(k, first, second):
        CS[k] = jnp.where(row_of == 0, first, second)
        for i in others:
            cs_send(k, i).start()

    def cs_finish(k):
        total = jnp.zeros(far.shape[1:], F32)
        for i in others:
            cs_send(k, i).wait()
            distance = lax.abs(lax.rem(z - i + T, T) - z)
            total = total + jnp.where(distance >= 2, CSR[k, i - 1], 0.0)
        far[k] = total

    cs_start(0, nn(ones, pairs[0, 1]), nn(ones, pairs[1, 1]))

    def halo_kv(r):
        @pl.when(z > 0)
        def _():
            halo_left(r).wait_send()
            halo_right(r).wait_recv()

        @pl.when(z < T - 1)
        def _():
            halo_right(r).wait_send()
            halo_left(r).wait_recv()

        for t in (0, 2):
            norm_tile(r, t)
            key_values(r, t)

    loop(rows, halo_kv)
    to_3(1, 2, 1)
    cs_finish(0)

    x_again = pltpu.make_async_copy(x_ref, act, lsem.at[4])
    x_again.start()

    def mixer(r):
        denom = nn(band[...], pairs[r, :, :, pl.ds(depth, depth)].reshape(3 * tile, depth))
        denom = denom + far[0, pl.ds(r, 1), pl.ds(depth, depth)]
        di = 1.0 / denom
        dinv[r] = di
        numer = nn(band[...], pairs[r, :, :, pl.ds(0, depth)].reshape(3 * tile, depth))
        rt = (numer + far[0, pl.ds(r, 1), pl.ds(0, depth)]) * di
        ratio[r] = rt
        mix[r] = (gates[r] * rt).astype(BF)

    loop(rows, mixer, lambda: middles(to_3, 2, 2, 1))
    ends(to_1, 2, 2, 1)
    x_again.wait()

    def middle(r):
        m = act[r].astype(F32) + nn(mix[r], mat(Wo))
        mid[r] = m
        gin_ref[r] = m
        xhat, _ = norm_parts(m)
        n2[r] = (xhat * gain2).astype(BF)
        gn2[r] = jnp.zeros((tile, depth), F32)

    loop(rows, middle)
    local[1].wait()
    local[2].wait()

    G = (W1, G1, G2)
    R = (W2, R1, R2)
    s1_base, s2_base, s3_base, sz_base, f_base = take(12), take(24), take(24), take(3 * T), take(15)
    early_base = take(2)
    def s1(g, o):
        j = slabs[o]
        return rc(G[g].at[j, :, :, 1 - c], R[g].at[j, :, :, 0], s1_base + g * 4 + o, core)

    def s1_kind(ty, tx):
        return rc(G[0].at[:, ty, tx, 1 - c], R[0].at[:, ty, tx, 0], s1_base + 2 * ty + tx, core)

    def s2(g, o, h):
        j = slabs[o]
        if h == 0:
            src, dst, dev = G[g].at[j, :, 1 - x, c, lo], R[g].at[j, 0, :, 1, lo], xp
        else:
            src, dst, dev = G[g].at[j, 1 - y, :, c, hi], R[g].at[j, 0, :, 1, hi], yp
        return rc(src, dst, s2_base + (g * 2 + h) * 4 + o, dev)

    def s2_early(h):
        if h == 0:
            src, dst, dev = G[0].at[:, 1 - x, 1 - x, c, lo], R[0].at[:, 0, 1 - x, 1, lo], xp
        else:
            src, dst, dev = G[0].at[:, 1 - y, 1 - y, c, hi], R[0].at[:, 0, 1 - y, 1, hi], yp
        return rc(src, dst, early_base + h, dev)

    def s2_late(o, h):
        j = slabs[o]
        if h == 0:
            src, dst, dev = G[0].at[j, x, 1 - x, c, lo], R[0].at[j, 0, x, 1, lo], xp
        else:
            src, dst, dev = G[0].at[j, 1 - y, y, c, hi], R[0].at[j, 0, y, 1, hi], yp
        return rc(src, dst, s2_base + h * 4 + o, dev)

    def s3(g, o, h):
        j = slabs[o]
        if h == 0:
            src, dst, dev = G[g].at[j, 1 - y, x, c, lo], R[g].at[j, 1, 0, 1, lo], yp
        else:
            src, dst, dev = G[g].at[j, y, 1 - x, c, hi], R[g].at[j, 1, 0, 1, hi], xp
        return rc(src, dst, s3_base + (g * 2 + h) * 4 + o, dev)

    pair = z + 1 - 2 * lax.rem(z, 2)
    across = lax.rem(z + 2, T)

    def sz_1(g, slot):
        j = lax.rem(pair + 2 * slot, T)
        return rc(G[g].at[j, y, x, c], R[g].at[slot, 1, 1, 1], sz_base + g * T + slot, (b, pair))

    def sz_2(g):
        return rc(G[g].at[across, y, x, c], R[g].at[2, 1, 1, 1], sz_base + g * T + 2, (b, across))

    def s1_finish(o, *groups):
        j = slabs[o]
        for g in groups:
            s1(g, o).wait()
            G[g][j, :, :, c] = G[g][j, :, :, c] + R[g][j, :, :, 0]
            for h in range(2):
                s2(g, o, h).start()

    def s1_kind_finish(ty, tx):
        s1_kind(ty, tx).wait()
        G[0][:, ty, tx, c] = G[0][:, ty, tx, c] + R[0][:, ty, tx, 0]

    def s2_finish(o, *groups):
        j = slabs[o]
        for g in groups:
            s2(g, o, 0).wait()
            G[g][j, :, x, c, lo] = G[g][j, :, x, c, lo] + R[g][j, 0, :, 1, lo]
            s3(g, o, 0).start()
            s2(g, o, 1).wait()
            G[g][j, y, :, c, hi] = G[g][j, y, :, c, hi] + R[g][j, 0, :, 1, hi]
            s3(g, o, 1).start()

    last_order = (1, 2, 3, 0)

    def s3_start(o):
        for h in range(2):
            s3(0, o, h).start()

    def s2_early_finish():
        for h in range(2):
            s2_early(h).wait()
        G[0][:, x, x, c, lo] = G[0][:, x, x, c, lo] + R[0][:, 0, x, 1, lo]
        G[0][:, y, y, c, hi] = G[0][:, y, y, c, hi] + R[0][:, 0, y, 1, hi]

        @pl.when(x != y)
        def _():
            for o in last_order:
                s3_start(o)

    def s2_late_finish(o):
        j = slabs[o]
        for h in range(2):
            s2_late(o, h).wait()
        G[0][j, 1 - x, x, c, lo] = G[0][j, 1 - x, x, c, lo] + R[0][j, 0, 1 - x, 1, lo]
        G[0][j, y, 1 - y, c, hi] = G[0][j, y, 1 - y, c, hi] + R[0][j, 0, 1 - y, 1, hi]
        pl.when(x == y)(lambda: s3_start(o))

    def s3_finish(o, *groups):
        j = slabs[o]
        for g in groups:
            s3(g, o, 0).wait()
            s3(g, o, 1).wait()
            G[g][j, y, x, c] = G[g][j, y, x, c] + R[g][j, 1, 0, 1]
            for slot in range(2):
                if o:
                    pl.when(j == lax.rem(pair + 2 * slot, T))(lambda: sz_1(g, slot).start())

    def f_at(g):
        return G[g].at[:, :, :, 1 - c]

    def f1(g, h):
        rng = (lo, hi)[h]
        other = f_at(g).at[c, y, x, rng]
        return rc(other, other, f_base + 5 * g + h, (xp, yp)[h])

    def f2(g, h):
        ref = f_at(g).at[c, y, :, lo] if h == 0 else f_at(g).at[c, :, x, hi]
        return rc(ref, ref, f_base + 5 * g + 2 + h, (yp, xp)[h])

    def f3(g):
        return rc(f_at(g).at[c], G[g].at[c, :, :, c], f_base + 5 * g + 4, core)

    u_base = take(4 * max(bits - 3, 0))

    def z_middle(g):
        sz_1(g, 1).wait()
        G[g][across, y, x, c] = G[g][across, y, x, c] + R[g][1, 1, 1, 1]
        sz_2(g).start()

    def z_finish(g):
        sz_1(g, 0).wait()
        sz_2(g).wait()
        total = G[g][z, y, x, c].astype(F32) + R[g][0, 1, 1, 1].astype(F32) + R[g][2, 1, 1, 1].astype(F32)
        mine = f_at(g).at[c, y, x]
        mine[...] = total.astype(BF)
        for k in range(3, bits):
            u = k - 3
            slot = f_at(g).at[2 + u // 4, u // 2 % 2, u % 2]
            pl.semaphore_signal(upper_ready.at[g, u], inc=1, device_id=flip(k), device_id_type=MESH)
            pl.semaphore_wait(upper_ready.at[g, u], 1)
            cp = rc(mine, slot, u_base + g * (bits - 3) + u, flip(k))
            cp.start()
            cp.wait()
            mine[...] = mine[...] + slot[...]
        for h in range(2):
            f1(g, h).start()

    def f1_finish(g):
        for h in range(2):
            f1(g, h).wait()
            f2(g, h).start()

    def f2_finish(g):
        for h in range(2):
            f2(g, h).wait()
        f3(g).start()

    def out_copies(g):
        pairs_of = []
        for k in range(2):
            if g:
                pairs_of.append((G[g].at[k, :, :, 1 - c], (f1_out, f2_out)[g - 1].at[:, :, k]))
                continue
            for ty in range(2):
                for tx in range(2):
                    dst = fo_out.at[k] if ty + tx == 2 else fq_out.at[2 * ty + tx, k]
                    pairs_of.append((G[0].at[k, ty, tx, 1 - c], dst))
        first = (5, 13, 15)[g]
        return [pltpu.make_async_copy(src, dst, lsem.at[first + i]) for i, (src, dst) in enumerate(pairs_of)]

    def f3_finish(g):
        f3(g).wait()
        for cp in out_copies(g):
            cp.start()

    def feed(o, between, after_sums):
        j = slabs[o]
        up, down = W1.at[j], W2.at[j]

        def part(r):
            for k in range(3):
                cols = pl.ds(k * (depth // 3), depth // 3)
                h = nn(n2[r], up[:, :, :, :, cols].reshape(depth, depth // 3))
                ga = nt(cot_ref[r], down[...].reshape(depth, depth)[k * (depth // 3) : (k + 1) * (depth // 3)])
                sq = h * h
                t = jnp.tanh(GELU_C * h * (1.0 + GELU_A * sq))
                hh = 0.5 * h
                act[r, :, cols] = (hh + hh * t).astype(BF)
                slope = 0.5 + 0.5 * t + hh * (1.0 - t * t) * (GELU_C + (3.0 * GELU_C * GELU_A) * sq)
                gh[r, :, cols] = (ga * slope).astype(BF)

        def collect(r):
            gin_ref[r] += nn(act[r], mat(down))
            gn2[r] += nt(gh[r], mat(up))

        loop(rows, part, between)
        for g, lhs, rhs in ((2, act, cot_ref), (1, n2, gh)):
            for m in range(2):
                cols = pl.ds(m * (depth // 2), depth // 2)
                d = tn(lhs[:, :, cols].reshape(rows * tile, depth // 2), rhs[...].reshape(rows * tile, depth))
                G[g][j, m] = d.astype(BF).reshape(2, 2, piece, depth)
            s1(g, o).start()
        after_sums()
        loop(rows, collect)
        s1_finish(o, 2, 1)

    def nothing():
        return

    feed(0, lambda: middles(to_1, 3, 2, 1), lambda: ends(to_2, 2, 2, 1))
    arrived(1, 2, 1)

    def second_between():
        middles(to_2, 3, 2, 1)
        ends(to_3, 2, 2, 1)
        ends(to_1, 3, 2, 1)

    def second_sums():
        middles(to_3, 3, 2, 1)
        ends(to_2, 3, 2, 1)

    feed(1, second_between, second_sums)
    arrived(2, 2, 1)
    feed(2, lambda: ends(to_3, 3, 2, 1), nothing)
    arrived(3, 2, 1)
    z_sent(0, 1, 2)
    feed(3, lambda: s2_finish(1, 2, 1), nothing)
    for dev in partners:
        pl.semaphore_signal(ready, inc=1, device_id=dev, device_id_type=MESH)

    def norm_two_back(r, carry):
        mixed_ref[r] = gin_ref[r].astype(BF)
        xhat, rstd = norm_parts(mid[r])
        grad = gn2[r]
        carry = carry + jnp.sum(grad * xhat, axis=0, keepdims=True)
        g = grad * gain2
        back = g - jnp.mean(g, axis=-1, keepdims=True) - xhat * jnp.mean(g * xhat, axis=-1, keepdims=True)
        gm = cot_ref[r].astype(F32) + rstd * back
        mid[r] = gm
        n2[r] = gm.astype(BF)
        return carry

    gain2_grad = lax.fori_loop(0, rows, norm_two_back, jnp.zeros((1, depth), F32))

    s2_finish(2, 2, 1)
    pl.semaphore_wait(ready, len(partners))

    local[3].start()

    def kind(ty, tx, lhs, start, rhs):
        for m in range(2):
            part = lhs[..., pl.ds(start + m * (depth // 2), depth // 2)]
            d = tn(part.reshape(rhs.shape[0], depth // 2), rhs).astype(BF)
            d = d.reshape(2, 2, piece, depth)
            for s in range(2):
                G[0][2 * m + s, ty, tx] = d[s]
        s1_kind(ty, tx).start()

    flat = (rows * tile, depth)
    kind(1, 1, mix, 0, n2[...].reshape(flat))
    s3_finish(1, 2, 1)

    def mixer_back(r):
        gmix = nt(n2[r], mat(Wo))
        gate = gates[r]
        rt = ratio[r]
        first = gmix * gate
        act[r] = (first * rt * (1.0 - gate)).astype(BF)
        first = first * dinv[r]
        gs[r, :, pl.ds(0, depth)] = first.astype(BF)
        gs[r, :, pl.ds(depth, depth)] = (-first * rt).astype(BF)

    loop(rows, mixer_back)
    cs_start(1, nn(ones, gs[0]), nn(ones, gs[1]))
    s2_finish(3, 2, 1)
    kind(0, 0, act, 0, n1[:, 1].reshape(flat))
    s3_finish(2, 2, 1)

    local[3].wait()
    gband = nt(gs[0], pairs[0].reshape(3 * tile, 2 * depth)) + nt(gs[1], pairs[1].reshape(3 * tile, 2 * depth))
    shift = lax.broadcasted_iota(jnp.int32, (tile, 1), 0)
    k = 1
    while k < tile:
        gband = jnp.where(lax.rem(shift // k, 2) == 1, pltpu.roll(gband, 3 * tile - k, 1), gband)
        k *= 2
    gp = (gband[:, :window] * jnp.exp(bias[...])).astype(BF)
    GP[...] = gp.reshape(GP.shape)
    p_base = take(6 + T)
    up_base = u_base + 3 * max(bits - 3, 0)

    def p1():
        return rc(GP.at[:, :, 1 - c], RP.at[:, :, 0], p_base, core)

    def p2():
        return rc(GP.at[:, 1 - x, c], RP.at[0, :, 1], p_base + 1, xp)

    def p3():
        return rc(GP.at[1 - y, x, c], RP.at[1, 0, 1], p_base + 2, yp)

    def pz(i):
        mine = FP.at[z, y, x, c]
        return rc(mine, mine, p_base + 6 + i, (b, slab(i)))

    def pa1():
        ref = FP.at[:, y, x, c]
        return rc(ref, ref, p_base + 3, xp)

    def pa2():
        ref = FP.at[:, y, :, c]
        return rc(ref, ref, p_base + 4, yp)

    def pa3():
        ref = FP.at[:, :, :, c]
        return rc(ref, ref, p_base + 5, core)

    p1().start()
    s1_kind_finish(1, 1)
    s1_kind_finish(0, 0)
    for h in range(2):
        s2_early(h).start()
    cs_finish(1)

    def pairs_back(r):
        for t in range(3):
            near = band[:, pl.ds(t * tile, tile)]
            gn = tn(near, gs[r, :, pl.ds(0, depth)])
            gd = tn(near, gs[r, :, pl.ds(depth, depth)])
            if t == 1:
                gn = gn + far[1, pl.ds(r, 1), pl.ds(0, depth)]
                gd = gd + far[1, pl.ds(r, 1), pl.ds(depth, depth)]
            wv = pairs[r, t, :, pl.ds(0, depth)].astype(F32)
            we = pairs[r, t, :, pl.ds(depth, depth)].astype(F32)
            pairs[r, t, :, pl.ds(0, depth)] = (gn * wv + gd * we).astype(BF)
            pairs[r, t, :, pl.ds(depth, depth)] = (gn * we).astype(BF)

    loop(rows, pairs_back, lambda: s3_finish(3, 2, 1))
    p1().wait()
    GP[:, :, c] = GP[:, :, c] + RP[:, :, 0]
    p2().start()
    n1_all = n1[...].reshape(3 * rows * tile, depth)
    kind(0, 1, pairs, 0, n1_all)
    s2_finish(0, 2, 1)
    z_middle(2)
    z_middle(1)
    kind(1, 0, pairs, depth, n1_all)
    s1_kind_finish(0, 1)

    def halo_part(d):
        def body(r):
            g = nn(pairs[r, 2 * d, :, pl.ds(0, depth)], mat(Wk))
            g = g + nn(pairs[r, 2 * d, :, pl.ds(depth, depth)], mat(Wv))
            gs[r, :, pl.ds(d * depth, depth)] = g.astype(BF)

        loop(rows, body)

    def back_left():
        return rc(gs.at[:, :, pl.ds(0, depth)], hr.at[1], halo_base, left)

    def back_right():
        return rc(gs.at[:, :, pl.ds(depth, depth)], hr.at[0], halo_base + 1, right)

    halo_part(0)
    pl.when(has_left)(lambda: back_left().start())
    s1_kind_finish(1, 0)
    for o in last_order:
        for h in range(2):
            s2_late(o, h).start()
    halo_part(1)
    pl.when(has_right)(lambda: back_right().start())
    p2().wait()
    GP[:, x, c] = GP[:, x, c] + RP[0, :, 1]
    p3().start()
    s2_early_finish()
    s3_finish(0, 2, 1)

    def own_grad(r):
        g = nn(act[r], mat(Wq)) + nn(pairs[r, 1, :, pl.ds(0, depth)], mat(Wk))
        gin_ref[r] = g + nn(pairs[r, 1, :, pl.ds(depth, depth)], mat(Wv))

    loop(rows, own_grad)
    x_again.start()
    for o in last_order:
        s2_late_finish(o)
    p3().wait()
    GP[y, x, c] = GP[y, x, c] + RP[1, 0, 1]
    for k in range(3, bits):
        cp = rc(GP.at[y, x, c], UPP.at[k - 3], up_base + k - 3, flip(k))
        cp.start()
        cp.wait()
        GP[y, x, c] = GP[y, x, c] + UPP[k - 3]
    FP[z, y, x, c] = GP[y, x, c]
    for i in others:
        pz(i).start()
    z_finish(2)
    z_finish(1)
    for i in others:
        pz(i).wait()
    pa1().start()
    for o in last_order:
        s3_finish(o, 0)
    f1_finish(2)
    f1_finish(1)
    z_middle(0)
    pa1().wait()
    pa2().start()

    pl.when(z > 0)(lambda: back_left().wait_send())
    pl.when(z < T - 1)(lambda: back_right().wait_send())
    pl.when(z < T - 1)(lambda: back_left().wait_recv())
    pl.when(z > 0)(lambda: back_right().wait_recv())
    x_again.wait()

    def norm_one_back(r, carry):
        xhat, rstd = norm_parts(act[r].astype(F32))
        grad = gin_ref[r] + hr[0, r].astype(F32) + hr[1, r].astype(F32)
        carry = carry + jnp.sum(grad * xhat, axis=0, keepdims=True)
        g = grad * gain1
        back = g - jnp.mean(g, axis=-1, keepdims=True) - xhat * jnp.mean(g * xhat, axis=-1, keepdims=True)
        gin_ref[r] = mid[r] + rstd * back
        return carry

    gain1_grad = lax.fori_loop(0, rows, norm_one_back, jnp.zeros((1, depth), F32))

    g_base = take(bits + T)
    GA[0] = jnp.where(row_of == 0, gain1_grad, gain2_grad)

    def ga(k):
        return rc(GA.at[k], GR.at[k], g_base + k, flip(k))

    def gz(i):
        return rc(GA.at[bits], GR.at[bits + z], g_base + bits + i, (b, slab(i)))

    def gains_step(k):
        ga(k).wait()
        GA[k + 1] = GA[k] + GR[k]
        if k + 1 < bits:
            ga(k + 1).start()
        else:
            GR[bits + z] = GA[bits]
            for i in others:
                gz(i).start()

    ga(0).start()
    f2_finish(2)
    f2_finish(1)
    gains_step(0)
    z_finish(0)
    pa2().wait()
    pa3().start()
    gains_step(1)
    f1_finish(0)
    gains_step(2)
    for k in range(3, bits):
        gains_step(k)
    f3_finish(2)
    f3_finish(1)
    f2_finish(0)
    for i in others:
        gz(i).wait()
    total = GR[bits]
    for i in range(1, T):
        total = total + GR[bits + i]
    gains1_ref[...] = total[0:1]
    gains2_ref[...] = total[1:2]
    pa3().wait()
    fp_copy = pltpu.make_async_copy(FP, fp_out, lsem.at[3])
    fp_copy.start()
    f3_finish(0)
    for g in range(3):
        for cp in out_copies(g):
            cp.wait()
    fp_copy.wait()


def per_device(
    tiles,
    batch,
    inputs,
    lengths,
    gain_one,
    qkv_weight,
    out_weight,
    gain_two,
    up_projection_weight,
    down_projection_weight,
    pair_bias,
    cotangent,
):
    tile, rows, depth = inputs.shape
    bits = batch.bit_length() - 1
    channels = qkv_weight.shape[2]
    piece = depth // 8
    window = pair_bias.shape[1]
    strip = tile // 8
    x = jnp.transpose(inputs, (1, 0, 2))
    cot = jnp.transpose(cotangent, (1, 0, 2))
    cut = (2, 2, 2, piece, depth)
    w0 = jnp.concatenate([jnp.transpose(qkv_weight, (0, 2, 1)), out_weight[None]]).reshape(cut)
    w1 = up_projection_weight.reshape(cut)
    w2 = down_projection_weight.reshape(cut)
    n_sems = 256 if bits == 3 else 288
    tokens = (rows, tile, depth)
    T = tiles
    vmem = pl.BlockSpec(memory_space=pltpu.VMEM)
    hbm = pl.BlockSpec(memory_space=pl.ANY)
    blocks = (T, 2, 2, 2, piece, depth)
    upper = max(bits - 3, 1)
    scratch = [
        pltpu.VMEM((2, 2, T, 2, piece, depth), BF),
        pltpu.VMEM(blocks, BF),
        pltpu.VMEM(blocks, BF),
        pltpu.VMEM(blocks, BF),
        pltpu.VMEM(blocks, BF),
        pltpu.VMEM(blocks, BF),
        pltpu.VMEM(blocks, BF),
        pltpu.VMEM((rows, 3, tile, depth), BF),
        pltpu.VMEM((rows, 3, tile, 2 * depth), BF),
        pltpu.VMEM(tokens, F32),
        pltpu.VMEM(tokens, F32),
        pltpu.VMEM(tokens, F32),
        pltpu.VMEM(tokens, F32),
        pltpu.VMEM(tokens, BF),
        pltpu.VMEM(tokens, BF),
        pltpu.VMEM(tokens, BF),
        pltpu.VMEM((rows, tile, 2 * depth), BF),
        pltpu.VMEM(tokens, F32),
        pltpu.VMEM((2,) + tokens, BF),
        pltpu.VMEM((tile, 3 * tile), BF),
        pltpu.VMEM((2, 2, 2, strip, window), BF),
        pltpu.VMEM((2, 2, 2, strip, window), BF),
        pltpu.VMEM((T, 2, 2, 2, strip, window), BF),
        pltpu.VMEM((2, 8, 2 * depth), F32),
        pltpu.VMEM((2, T - 1, 8, 2 * depth), F32),
        pltpu.VMEM((2, 8, 2 * depth), F32),
        pltpu.VMEM((bits + 1, 8, depth), F32),
        pltpu.VMEM((bits + T, 8, depth), F32),
        pltpu.VMEM((upper, strip, window), BF),
        pltpu.SemaphoreType.DMA((n_sems,)),
        pltpu.SemaphoreType.DMA((n_sems,)),
        pltpu.SemaphoreType.DMA((17,)),
        pltpu.SemaphoreType.REGULAR,
        pltpu.SemaphoreType.REGULAR((3, upper)),
    ]
    mixed, grad_inputs, gains1, gains2, fq, fo, f1, f2, pair = pl.pallas_call(
        functools.partial(kernel, T, bits, T * tile, n_sems),
        out_shape=(
            jax.ShapeDtypeStruct(tokens, BF),
            jax.ShapeDtypeStruct(tokens, F32),
            jax.ShapeDtypeStruct((1, depth), F32),
            jax.ShapeDtypeStruct((1, depth), F32),
            jax.ShapeDtypeStruct((3, 2, piece, depth), BF),
            jax.ShapeDtypeStruct((2, piece, depth), BF),
            jax.ShapeDtypeStruct(cut, BF),
            jax.ShapeDtypeStruct(cut, BF),
            jax.ShapeDtypeStruct((T, 2, 2, 2, strip, window), BF),
        ),
        in_specs=[pl.BlockSpec(memory_space=pltpu.SMEM), hbm, vmem, vmem, hbm, hbm, hbm, hbm],
        out_specs=(vmem, vmem, vmem, vmem, hbm, hbm, hbm, hbm, hbm),
        scratch_shapes=scratch,
        compiler_params=pltpu.CompilerParams(
            collective_id=0, has_side_effects=True, vmem_limit_bytes=VMEM_BYTES
        ),
    )(
        lengths,
        x,
        cot,
        jnp.stack([gain_one, gain_two]).astype(F32),
        w0,
        w1,
        w2,
        pair_bias,
    )
    turned = lax.optimization_barrier(jnp.transpose(fq.reshape(3, channels, depth), (0, 2, 1)))
    return (
        jnp.transpose(mixed, (1, 0, 2)),
        jnp.transpose(grad_inputs, (1, 0, 2)),
        gains1.reshape(depth),
        turned.astype(F32),
        fo.reshape(channels, depth).astype(F32),
        gains2.reshape(depth),
        f1.reshape(depth, depth).astype(F32),
        f2.reshape(depth, depth).astype(F32),
        pair.reshape(T * tile, window).astype(F32),
    )


def solution(mesh):
    return jax.shard_map(
        functools.partial(per_device, mesh.shape["tensor"], mesh.shape["batch"]),
        mesh=mesh,
        in_specs=(
            P("tensor", "batch", None),
            P("batch"),
            P(),
            P(None, None, "tensor"),
            P("tensor", None),
            P(),
            P(None, "tensor"),
            P("tensor", None),
            P(),
            P("tensor", "batch", None),
        ),
        out_specs=(
            P("tensor", "batch", None),
            P("tensor", "batch", None),
            P(),
            P(None, None, "tensor"),
            P("tensor", None),
            P(),
            P(None, "tensor"),
            P("tensor", None),
            P(),
        ),
        check_vma=False,
    )
```

```python
import functools

import jax
import jax.numpy as jnp
from jax import lax
from jax.experimental import pallas as pl
from jax.experimental.pallas import tpu as pltpu
from jax.sharding import PartitionSpec as P

MESH = pl.DeviceIdType.MESH
BF = jnp.bfloat16
F32 = jnp.float32
GELU_A = 0.044715
GELU_C = 0.7978845608028654
VMEM_BYTES = 63 << 20


def dot(a, b, ca, cb):
    return lax.dot_general(a, b, (((ca,), (cb,)), ((), ())), preferred_element_type=F32)


def nn(a, b):
    return dot(a, b, 1, 0)


def nt(a, b):
    return dot(a, b, 1, 1)


def tn(a, b):
    return dot(a, b, 0, 0)


def norm_parts(v):
    shifted = v - jnp.mean(v, axis=-1, keepdims=True)
    rstd = lax.rsqrt(jnp.mean(shifted * shifted, axis=-1, keepdims=True) + 1e-05)
    return shifted * rstd, rstd


def kernel(
    tiles,
    bits,
    length,
    n_sems,
    len_ref,
    x_ref,
    cot_ref,
    gain_ref,
    w0_in,
    w1_in,
    w2_in,
    bias_in,
    mixed_ref,
    gin_ref,
    gains1_ref,
    gains2_ref,
    fq_out,
    fo_out,
    f1_out,
    f2_out,
    fp_out,
    W0,
    W1,
    W2,
    G1,
    G2,
    R1,
    R2,
    n1,
    pairs,
    gates,
    ratio,
    dinv,
    mid,
    act,
    n2,
    mix,
    gs,
    gn2,
    hr,
    band,
    GP,
    RP,
    FP,
    CS,
    CSR,
    far,
    GA,
    GR,
    UPP,
    ssem,
    rsem,
    lsem,
    ready,
    upper_ready,
):
    T = tiles
    rows, tile, depth = cot_ref.shape
    piece = W1.shape[4]
    half = piece // 2
    b = lax.axis_index("batch")
    z = lax.axis_index("tensor")
    c = lax.rem(b, 2)
    x = lax.rem(b // 2, 2)
    y = lax.rem(b // 4, 2)
    gh = mixed_ref

    def flip(k):
        q = lax.rem(b // (1 << k), 2)
        return (b + (1 << k) - 2 * (1 << k) * q, z)

    core, xp, yp = flip(0), flip(1), flip(2)
    counter = [0]

    def take(n):
        counter[0] += n
        assert counter[0] <= n_sems
        return counter[0] - n

    def rc(src, dst, sem, dev, sent=None):
        return pltpu.make_async_remote_copy(
            src_ref=src,
            dst_ref=dst,
            send_sem=ssem.at[sem if sent is None else sent],
            recv_sem=rsem.at[sem],
            device_id=dev,
            device_id_type=MESH,
        )

    def slab(i):
        return lax.rem(z + i, T)

    def nth(k):
        near = [sorted(range(T), key=lambda j: (abs(j - q), j))[k] for q in range(T)]
        return sum(near[q] * (1 - lax.min(lax.abs(z - q), 1)) for q in range(T))

    slabs = [z] + [nth(k) for k in range(1, T)]
    lo, hi = pl.ds(0, half), pl.ds(half, half)
    partners = [flip(k) for k in range(bits)] + [(b, slab(i)) for i in range(1, T)]

    def w_at(g, j):
        return W0.at[:, :, j] if g == 0 else (W1, W2)[g - 1].at[j]

    w_in = (w0_in, w1_in, w2_in)
    local = [pltpu.make_async_copy(w_in[g], w_at(g, z), lsem.at[g]) for g in range(3)]
    window = bias_in.shape[1]
    bias = gn2.at[0, :, pl.ds(0, window)]
    local.append(pltpu.make_async_copy(bias_in.at[pl.ds(z * tile, tile)], bias, lsem.at[3]))
    local.append(pltpu.make_async_copy(x_ref, n1.at[:, 1], lsem.at[4]))
    for cp in local:
        cp.start()

    barrier = pltpu.get_barrier_semaphore()
    for dev in partners:
        pl.semaphore_signal(barrier, inc=1, device_id=dev, device_id_type=MESH)
    pl.semaphore_wait(barrier, len(partners))

    z_base, a1_base, a2_base, a3_base = take(3 * T), take(6 * T), take(6 * T), take(3 * T)
    own_base = take(6)
    right, left = (b, lax.min(z + 1, T - 1)), (b, lax.max(z - 1, 0))
    has_right, has_left = z < T - 1, z > 0

    def piece_at(g, j):
        return W0.at[y, x, j, c] if g == 0 else (W1, W2)[g - 1].at[j, y, x, c]

    def own_send(g, side):
        dst = piece_at(g, z)
        return rc(w_in[g].at[y, x, c], dst, z_base + g * T + z, (right, left)[side], own_base + 2 * g + side)

    def pass_on(g, k, side):
        ref = piece_at(g, slabs[k])
        return rc(ref, ref, z_base + g * T + slabs[k], (right, left)[side])

    def ag_1(g, k, h):
        ref = piece_at(g, slabs[k]).at[(lo, hi)[h]]
        return rc(ref, ref, a1_base + (g * 2 + h) * T + k, (xp, yp)[h])

    def ag_2(g, k, h):
        j = slabs[k]
        W = (W0, W1, W2)[g]
        if h == 0:
            ref = W.at[y, :, j, c, lo] if g == 0 else W.at[j, y, :, c, lo]
        else:
            ref = W.at[:, x, j, c, hi] if g == 0 else W.at[j, :, x, c, hi]
        return rc(ref, ref, a2_base + (g * 2 + h) * T + k, (yp, xp)[h])

    def ag_3(g, k):
        j = slabs[k]
        ref = W0.at[:, :, j, c] if g == 0 else (W1, W2)[g - 1].at[j, :, :, c]
        return rc(ref, ref, a3_base + g * T + k, core)

    others = range(1, T)

    def z_start(*groups):
        for side, there in ((0, has_right), (1, has_left)):

            @pl.when(there)
            def _():
                for g in groups:
                    own_send(g, side).start()

    def passing(k):
        j = slabs[k]
        return ((0, (j < z) & has_right), (1, (j > z) & has_left))

    def to_1(k, *groups):
        for g in groups:
            pass_on(g, k, 0).wait_recv()
            for side, there in passing(k):
                pl.when(there)(lambda: pass_on(g, k, side).start())
            for h in range(2):
                ag_1(g, k, h).start()

    def to_2(k, *groups):
        for g in groups:
            for h in range(2):
                ag_1(g, k, h).wait()
                ag_2(g, k, h).start()

    def to_3(k, *groups):
        for g in groups:
            for h in range(2):
                ag_2(g, k, h).wait()
            ag_3(g, k).start()

    def arrived(k, *groups):
        for g in groups:
            ag_3(g, k).wait()
            for side, there in passing(k):
                pl.when(there)(lambda: pass_on(g, k, side).wait_send())

    def z_sent(*groups):
        for side, there in ((0, has_right), (1, has_left)):

            @pl.when(there)
            def _():
                for g in groups:
                    own_send(g, side).wait_send()

    halo_base = take(2 * rows + 2)

    def halo_right(r):
        return rc(x_ref.at[r], n1.at[r, 0], halo_base + 2 + 2 * r, right)

    def halo_left(r):
        return rc(x_ref.at[r], n1.at[r, 2], halo_base + 3 + 2 * r, left)

    z_start(0)

    @pl.when(z == 0)
    def _():
        n1[:, 0] = jnp.zeros((rows, tile, depth), BF)
        hr[0] = jnp.zeros((rows, tile, depth), BF)

    @pl.when(z == T - 1)
    def _():
        n1[:, 2] = jnp.zeros((rows, tile, depth), BF)
        hr[1] = jnp.zeros((rows, tile, depth), BF)

    gain1 = gain_ref[0:1]
    gain2 = gain_ref[1:2]

    def loop(n, body, between=None):
        def step(i, carry):
            body(i)
            if between is not None:
                pl.when(i == 0)(between)
            return carry

        lax.fori_loop(0, n, step, 0)

    def norm_tile(r, t):
        xhat, _ = norm_parts(n1[r, t].astype(F32))
        n1[r, t] = (xhat * gain1).astype(BF)

    local[3].wait()
    wide = jnp.concatenate([jnp.exp(bias[...]), jnp.ones((tile, 3 * tile - window), F32)], axis=1)
    band[...] = pltpu.roll(wide, 0, 1, stride=1, stride_axis=0).astype(BF)
    local[4].wait()
    loop(rows, lambda r: norm_tile(r, 1))

    def mat(ref):
        return ref[...].reshape(depth, depth)

    Wq, Wk, Wv, Wo = W0.at[0, 0], W0.at[0, 1], W0.at[1, 0], W0.at[1, 1]

    def halo_start(r):
        pl.when(has_right)(lambda: halo_right(r).start())
        pl.when(has_left)(lambda: halo_left(r).start())

    at_end = (z == 0) | (z == T - 1)

    inside = z * (T - 1 - z) > 0

    def ends(step, *args):
        pl.when(at_end)(lambda: step(*args))

    def middles(step, *args):
        pl.when(inside)(lambda: step(*args))

    @pl.when(at_end)
    def _():
        halo_start(0)
        z_start(2, 1)
        for r in range(1, rows):
            halo_start(r)

    to_1(1, 0)
    to_1(2, 0)
    to_2(1, 0)
    to_1(3, 0)

    @pl.when(inside)
    def _():
        halo_start(0)
        z_start(2, 1)
        for r in range(1, rows):
            halo_start(r)

    to_2(2, 0)
    to_3(1, 0)
    to_2(3, 0)
    to_3(2, 0)
    to_1(1, 2, 1)
    middles(to_1, 2, 2, 1)
    to_3(3, 0)
    for k in others:
        arrived(k, 0)
    local[0].wait()

    def key_values(r, t):
        n = n1[r, t]
        pos = (z - 1 + t) * tile + lax.broadcasted_iota(jnp.int32, (tile, 1), 0)
        keep = (pos >= 0) & (pos < length) & (pos < len_ref[r])
        e = jnp.where(keep, jnp.exp(nt(n, mat(Wk))), 0.0)
        v = nt(n, mat(Wv))
        pairs[r, t, :, pl.ds(0, depth)] = (e * v).astype(BF)
        pairs[r, t, :, pl.ds(depth, depth)] = e.astype(BF)

    def own_qkv(r):
        gates[r] = jax.nn.sigmoid(nt(n1[r, 1], mat(Wq)))
        key_values(r, 1)

    loop(rows, own_qkv, lambda: to_2(1, 2, 1))
    middles(to_2, 2, 2, 1)

    ones = jnp.ones((8, tile), BF)
    row_of = lax.broadcasted_iota(jnp.int32, (8, 1), 0)
    cs_base = take(2 * T)

    def cs_send(k, i):
        return rc(CS.at[k], CSR.at[k, i - 1], cs_base + k * T + i, (b, slab(i)))

    def cs_start(k, first, second):
        CS[k] = jnp.where(row_of == 0, first, second)
        for i in others:
            cs_send(k, i).start()

    def cs_finish(k):
        total = jnp.zeros(far.shape[1:], F32)
        for i in others:
            cs_send(k, i).wait()
            distance = lax.abs(lax.rem(z - i + T, T) - z)
            total = total + jnp.where(distance >= 2, CSR[k, i - 1], 0.0)
        far[k] = total

    cs_start(0, nn(ones, pairs[0, 1]), nn(ones, pairs[1, 1]))

    def halo_kv(r):
        @pl.when(z > 0)
        def _():
            halo_left(r).wait_send()
            halo_right(r).wait_recv()

        @pl.when(z < T - 1)
        def _():
            halo_right(r).wait_send()
            halo_left(r).wait_recv()

        for t in (0, 2):
            norm_tile(r, t)
            key_values(r, t)

    loop(rows, halo_kv)
    to_3(1, 2, 1)
    cs_finish(0)

    x_again = pltpu.make_async_copy(x_ref, act, lsem.at[4])
    x_again.start()

    def mixer(r):
        denom = nn(band[...], pairs[r, :, :, pl.ds(depth, depth)].reshape(3 * tile, depth))
        denom = denom + far[0, pl.ds(r, 1), pl.ds(depth, depth)]
        di = 1.0 / denom
        dinv[r] = di
        numer = nn(band[...], pairs[r, :, :, pl.ds(0, depth)].reshape(3 * tile, depth))
        rt = (numer + far[0, pl.ds(r, 1), pl.ds(0, depth)]) * di
        ratio[r] = rt
        mix[r] = (gates[r] * rt).astype(BF)

    loop(rows, mixer, lambda: middles(to_3, 2, 2, 1))
    ends(to_1, 2, 2, 1)
    x_again.wait()

    def middle(r):
        m = act[r].astype(F32) + nn(mix[r], mat(Wo))
        mid[r] = m
        gin_ref[r] = m
        xhat, _ = norm_parts(m)
        n2[r] = (xhat * gain2).astype(BF)
        gn2[r] = jnp.zeros((tile, depth), F32)

    loop(rows, middle)
    local[1].wait()
    local[2].wait()

    G = (W1, G1, G2)
    R = (W2, R1, R2)
    s1_base, s2_base, s3_base, sz_base, f_base = take(12), take(24), take(24), take(3 * T), take(15)
    early_base = take(2)
    def s1(g, o):
        j = slabs[o]
        return rc(G[g].at[j, :, :, 1 - c], R[g].at[j, :, :, 0], s1_base + g * 4 + o, core)

    def s1_kind(ty, tx):
        return rc(G[0].at[:, ty, tx, 1 - c], R[0].at[:, ty, tx, 0], s1_base + 2 * ty + tx, core)

    def s2(g, o, h):
        j = slabs[o]
        if h == 0:
            src, dst, dev = G[g].at[j, :, 1 - x, c, lo], R[g].at[j, 0, :, 1, lo], xp
        else:
            src, dst, dev = G[g].at[j, 1 - y, :, c, hi], R[g].at[j, 0, :, 1, hi], yp
        return rc(src, dst, s2_base + (g * 2 + h) * 4 + o, dev)

    def s2_early(h):
        if h == 0:
            src, dst, dev = G[0].at[:, 1 - x, 1 - x, c, lo], R[0].at[:, 0, 1 - x, 1, lo], xp
        else:
            src, dst, dev = G[0].at[:, 1 - y, 1 - y, c, hi], R[0].at[:, 0, 1 - y, 1, hi], yp
        return rc(src, dst, early_base + h, dev)

    def s2_late(o, h):
        j = slabs[o]
        if h == 0:
            src, dst, dev = G[0].at[j, x, 1 - x, c, lo], R[0].at[j, 0, x, 1, lo], xp
        else:
            src, dst, dev = G[0].at[j, 1 - y, y, c, hi], R[0].at[j, 0, y, 1, hi], yp
        return rc(src, dst, s2_base + h * 4 + o, dev)

    def s3(g, o, h):
        j = slabs[o]
        if h == 0:
            src, dst, dev = G[g].at[j, 1 - y, x, c, lo], R[g].at[j, 1, 0, 1, lo], yp
        else:
            src, dst, dev = G[g].at[j, y, 1 - x, c, hi], R[g].at[j, 1, 0, 1, hi], xp
        return rc(src, dst, s3_base + (g * 2 + h) * 4 + o, dev)

    pair = z + 1 - 2 * lax.rem(z, 2)
    across = lax.rem(z + 2, T)

    def sz_1(g, slot):
        j = lax.rem(pair + 2 * slot, T)
        return rc(G[g].at[j, y, x, c], R[g].at[slot, 1, 1, 1], sz_base + g * T + slot, (b, pair))

    def sz_2(g):
        return rc(G[g].at[across, y, x, c], R[g].at[2, 1, 1, 1], sz_base + g * T + 2, (b, across))

    def s1_finish(o, *groups):
        j = slabs[o]
        for g in groups:
            s1(g, o).wait()
            G[g][j, :, :, c] = G[g][j, :, :, c] + R[g][j, :, :, 0]
            for h in range(2):
                s2(g, o, h).start()

    def s1_kind_finish(ty, tx):
        s1_kind(ty, tx).wait()
        G[0][:, ty, tx, c] = G[0][:, ty, tx, c] + R[0][:, ty, tx, 0]

    def s2_finish(o, *groups):
        j = slabs[o]
        for g in groups:
            s2(g, o, 0).wait()
            G[g][j, :, x, c, lo] = G[g][j, :, x, c, lo] + R[g][j, 0, :, 1, lo]
            s3(g, o, 0).start()
            s2(g, o, 1).wait()
            G[g][j, y, :, c, hi] = G[g][j, y, :, c, hi] + R[g][j, 0, :, 1, hi]
            s3(g, o, 1).start()

    last_order = (1, 2, 3, 0)

    def s3_start(o):
        for h in range(2):
            s3(0, o, h).start()

    def s2_early_finish():
        for h in range(2):
            s2_early(h).wait()
        G[0][:, x, x, c, lo] = G[0][:, x, x, c, lo] + R[0][:, 0, x, 1, lo]
        G[0][:, y, y, c, hi] = G[0][:, y, y, c, hi] + R[0][:, 0, y, 1, hi]

        @pl.when(x != y)
        def _():
            for o in last_order:
                s3_start(o)

    def s2_late_finish(o):
        j = slabs[o]
        for h in range(2):
            s2_late(o, h).wait()
        G[0][j, 1 - x, x, c, lo] = G[0][j, 1 - x, x, c, lo] + R[0][j, 0, 1 - x, 1, lo]
        G[0][j, y, 1 - y, c, hi] = G[0][j, y, 1 - y, c, hi] + R[0][j, 0, 1 - y, 1, hi]
        pl.when(x == y)(lambda: s3_start(o))

    def s3_finish(o, *groups):
        j = slabs[o]
        for g in groups:
            s3(g, o, 0).wait()
            s3(g, o, 1).wait()
            G[g][j, y, x, c] = G[g][j, y, x, c] + R[g][j, 1, 0, 1]
            for slot in range(2):
                if o:
                    pl.when(j == lax.rem(pair + 2 * slot, T))(lambda: sz_1(g, slot).start())

    def f_at(g):
        return G[g].at[:, :, :, 1 - c]

    def f1(g, h):
        rng = (lo, hi)[h]
        other = f_at(g).at[c, y, x, rng]
        return rc(other, other, f_base + 5 * g + h, (xp, yp)[h])

    def f2(g, h):
        ref = f_at(g).at[c, y, :, lo] if h == 0 else f_at(g).at[c, :, x, hi]
        return rc(ref, ref, f_base + 5 * g + 2 + h, (yp, xp)[h])

    def f3(g):
        return rc(f_at(g).at[c], G[g].at[c, :, :, c], f_base + 5 * g + 4, core)

    u_base = take(4 * max(bits - 3, 0))

    def z_middle(g):
        sz_1(g, 1).wait()
        G[g][across, y, x, c] = G[g][across, y, x, c] + R[g][1, 1, 1, 1]
        sz_2(g).start()

    def z_finish(g):
        sz_1(g, 0).wait()
        sz_2(g).wait()
        total = G[g][z, y, x, c].astype(F32) + R[g][0, 1, 1, 1].astype(F32) + R[g][2, 1, 1, 1].astype(F32)
        mine = f_at(g).at[c, y, x]
        mine[...] = total.astype(BF)
        for k in range(3, bits):
            u = k - 3
            slot = f_at(g).at[2 + u // 4, u // 2 % 2, u % 2]
            pl.semaphore_signal(upper_ready.at[g, u], inc=1, device_id=flip(k), device_id_type=MESH)
            pl.semaphore_wait(upper_ready.at[g, u], 1)
            cp = rc(mine, slot, u_base + g * (bits - 3) + u, flip(k))
            cp.start()
            cp.wait()
            mine[...] = mine[...] + slot[...]
        for h in range(2):
            f1(g, h).start()

    def f1_finish(g):
        for h in range(2):
            f1(g, h).wait()
            f2(g, h).start()

    def f2_finish(g):
        for h in range(2):
            f2(g, h).wait()
        f3(g).start()

    def out_copies(g):
        pairs_of = []
        for k in range(2):
            if g:
                pairs_of.append((G[g].at[k, :, :, 1 - c], (f1_out, f2_out)[g - 1].at[:, :, k]))
                continue
            for ty in range(2):
                for tx in range(2):
                    dst = fo_out.at[k] if ty + tx == 2 else fq_out.at[2 * ty + tx, k]
                    pairs_of.append((G[0].at[k, ty, tx, 1 - c], dst))
        first = (5, 13, 15)[g]
        return [pltpu.make_async_copy(src, dst, lsem.at[first + i]) for i, (src, dst) in enumerate(pairs_of)]

    def f3_finish(g):
        f3(g).wait()
        for cp in out_copies(g):
            cp.start()

    def feed(o, between, after_sums):
        j = slabs[o]
        up, down = W1.at[j], W2.at[j]

        def part(r):
            for k in range(3):
                cols = pl.ds(k * (depth // 3), depth // 3)
                h = nn(n2[r], up[:, :, :, :, cols].reshape(depth, depth // 3))
                ga = nt(cot_ref[r], down[...].reshape(depth, depth)[k * (depth // 3) : (k + 1) * (depth // 3)])
                sq = h * h
                t = jnp.tanh(GELU_C * h * (1.0 + GELU_A * sq))
                hh = 0.5 * h
                act[r, :, cols] = (hh + hh * t).astype(BF)
                slope = 0.5 + 0.5 * t + hh * (1.0 - t * t) * (GELU_C + (3.0 * GELU_C * GELU_A) * sq)
                gh[r, :, cols] = (ga * slope).astype(BF)

        def collect(r):
            gin_ref[r] += nn(act[r], mat(down))
            gn2[r] += nt(gh[r], mat(up))

        loop(rows, part, between)
        for g, lhs, rhs in ((2, act, cot_ref), (1, n2, gh)):
            for m in range(2):
                cols = pl.ds(m * (depth // 2), depth // 2)
                d = tn(lhs[:, :, cols].reshape(rows * tile, depth // 2), rhs[...].reshape(rows * tile, depth))
                G[g][j, m] = d.astype(BF).reshape(2, 2, piece, depth)
            s1(g, o).start()
        after_sums()
        loop(rows, collect)
        s1_finish(o, 2, 1)

    def nothing():
        return

    feed(0, lambda: middles(to_1, 3, 2, 1), lambda: ends(to_2, 2, 2, 1))
    arrived(1, 2, 1)

    def second_between():
        middles(to_2, 3, 2, 1)
        ends(to_3, 2, 2, 1)
        ends(to_1, 3, 2, 1)

    def second_sums():
        middles(to_3, 3, 2, 1)
        ends(to_2, 3, 2, 1)

    feed(1, second_between, second_sums)
    arrived(2, 2, 1)
    feed(2, lambda: ends(to_3, 3, 2, 1), nothing)
    arrived(3, 2, 1)
    z_sent(0, 1, 2)
    feed(3, lambda: s2_finish(1, 2, 1), nothing)
    for dev in partners:
        pl.semaphore_signal(ready, inc=1, device_id=dev, device_id_type=MESH)

    def norm_two_back(r, carry):
        mixed_ref[r] = gin_ref[r].astype(BF)
        xhat, rstd = norm_parts(mid[r])
        grad = gn2[r]
        carry = carry + jnp.sum(grad * xhat, axis=0, keepdims=True)
        g = grad * gain2
        back = g - jnp.mean(g, axis=-1, keepdims=True) - xhat * jnp.mean(g * xhat, axis=-1, keepdims=True)
        gm = cot_ref[r].astype(F32) + rstd * back
        mid[r] = gm
        n2[r] = gm.astype(BF)
        return carry

    gain2_grad = lax.fori_loop(0, rows, norm_two_back, jnp.zeros((1, depth), F32))

    s2_finish(2, 2, 1)
    pl.semaphore_wait(ready, len(partners))

    local[3].start()

    def kind(ty, tx, lhs, start, rhs):
        for m in range(2):
            part = lhs[..., pl.ds(start + m * (depth // 2), depth // 2)]
            d = tn(part.reshape(rhs.shape[0], depth // 2), rhs).astype(BF)
            d = d.reshape(2, 2, piece, depth)
            for s in range(2):
                G[0][2 * m + s, ty, tx] = d[s]
        s1_kind(ty, tx).start()

    flat = (rows * tile, depth)
    kind(1, 1, mix, 0, n2[...].reshape(flat))
    s3_finish(1, 2, 1)

    def mixer_back(r):
        gmix = nt(n2[r], mat(Wo))
        gate = gates[r]
        rt = ratio[r]
        first = gmix * gate
        act[r] = (first * rt * (1.0 - gate)).astype(BF)
        first = first * dinv[r]
        gs[r, :, pl.ds(0, depth)] = first.astype(BF)
        gs[r, :, pl.ds(depth, depth)] = (-first * rt).astype(BF)

    loop(rows, mixer_back)
    cs_start(1, nn(ones, gs[0]), nn(ones, gs[1]))
    s2_finish(3, 2, 1)
    kind(0, 0, act, 0, n1[:, 1].reshape(flat))
    s3_finish(2, 2, 1)

    local[3].wait()
    gband = nt(gs[0], pairs[0].reshape(3 * tile, 2 * depth)) + nt(gs[1], pairs[1].reshape(3 * tile, 2 * depth))
    shift = lax.broadcasted_iota(jnp.int32, (tile, 1), 0)
    k = 1
    while k < tile:
        gband = jnp.where(lax.rem(shift // k, 2) == 1, pltpu.roll(gband, 3 * tile - k, 1), gband)
        k *= 2
    gp = (gband[:, :window] * jnp.exp(bias[...])).astype(BF)
    GP[...] = gp.reshape(GP.shape)
    p_base = take(6 + T)
    up_base = u_base + 3 * max(bits - 3, 0)

    def p1():
        return rc(GP.at[:, :, 1 - c], RP.at[:, :, 0], p_base, core)

    def p2():
        return rc(GP.at[:, 1 - x, c], RP.at[0, :, 1], p_base + 1, xp)

    def p3():
        return rc(GP.at[1 - y, x, c], RP.at[1, 0, 1], p_base + 2, yp)

    def pz(i):
        mine = FP.at[z, y, x, c]
        return rc(mine, mine, p_base + 6 + i, (b, slab(i)))

    def pa1():
        ref = FP.at[:, y, x, c]
        return rc(ref, ref, p_base + 3, xp)

    def pa2():
        ref = FP.at[:, y, :, c]
        return rc(ref, ref, p_base + 4, yp)

    def pa3():
        ref = FP.at[:, :, :, c]
        return rc(ref, ref, p_base + 5, core)

    p1().start()
    s1_kind_finish(1, 1)
    s1_kind_finish(0, 0)
    for h in range(2):
        s2_early(h).start()
    cs_finish(1)

    def pairs_back(r):
        for t in range(3):
            near = band[:, pl.ds(t * tile, tile)]
            gn = tn(near, gs[r, :, pl.ds(0, depth)])
            gd = tn(near, gs[r, :, pl.ds(depth, depth)])
            if t == 1:
                gn = gn + far[1, pl.ds(r, 1), pl.ds(0, depth)]
                gd = gd + far[1, pl.ds(r, 1), pl.ds(depth, depth)]
            wv = pairs[r, t, :, pl.ds(0, depth)].astype(F32)
            we = pairs[r, t, :, pl.ds(depth, depth)].astype(F32)
            pairs[r, t, :, pl.ds(0, depth)] = (gn * wv + gd * we).astype(BF)
            pairs[r, t, :, pl.ds(depth, depth)] = (gn * we).astype(BF)

    loop(rows, pairs_back, lambda: s3_finish(3, 2, 1))
    p1().wait()
    GP[:, :, c] = GP[:, :, c] + RP[:, :, 0]
    p2().start()
    n1_all = n1[...].reshape(3 * rows * tile, depth)
    kind(0, 1, pairs, 0, n1_all)
    s2_finish(0, 2, 1)
    z_middle(2)
    z_middle(1)
    kind(1, 0, pairs, depth, n1_all)
    s1_kind_finish(0, 1)

    def halo_part(d):
        def body(r):
            g = nn(pairs[r, 2 * d, :, pl.ds(0, depth)], mat(Wk))
            g = g + nn(pairs[r, 2 * d, :, pl.ds(depth, depth)], mat(Wv))
            gs[r, :, pl.ds(d * depth, depth)] = g.astype(BF)

        loop(rows, body)

    def back_left():
        return rc(gs.at[:, :, pl.ds(0, depth)], hr.at[1], halo_base, left)

    def back_right():
        return rc(gs.at[:, :, pl.ds(depth, depth)], hr.at[0], halo_base + 1, right)

    halo_part(0)
    pl.when(has_left)(lambda: back_left().start())
    s1_kind_finish(1, 0)
    for o in last_order:
        for h in range(2):
            s2_late(o, h).start()
    halo_part(1)
    pl.when(has_right)(lambda: back_right().start())
    p2().wait()
    GP[:, x, c] = GP[:, x, c] + RP[0, :, 1]
    p3().start()
    s2_early_finish()
    s3_finish(0, 2, 1)

    def own_grad(r):
        g = nn(act[r], mat(Wq)) + nn(pairs[r, 1, :, pl.ds(0, depth)], mat(Wk))
        gin_ref[r] = g + nn(pairs[r, 1, :, pl.ds(depth, depth)], mat(Wv))

    loop(rows, own_grad)
    x_again.start()
    for o in last_order:
        s2_late_finish(o)
    p3().wait()
    GP[y, x, c] = GP[y, x, c] + RP[1, 0, 1]
    for k in range(3, bits):
        cp = rc(GP.at[y, x, c], UPP.at[k - 3], up_base + k - 3, flip(k))
        cp.start()
        cp.wait()
        GP[y, x, c] = GP[y, x, c] + UPP[k - 3]
    FP[z, y, x, c] = GP[y, x, c]
    for i in others:
        pz(i).start()
    z_finish(2)
    z_finish(1)
    for i in others:
        pz(i).wait()
    pa1().start()
    for o in last_order:
        s3_finish(o, 0)
    f1_finish(2)
    f1_finish(1)
    z_middle(0)
    pa1().wait()
    pa2().start()

    pl.when(z > 0)(lambda: back_left().wait_send())
    pl.when(z < T - 1)(lambda: back_right().wait_send())
    pl.when(z < T - 1)(lambda: back_left().wait_recv())
    pl.when(z > 0)(lambda: back_right().wait_recv())
    x_again.wait()

    def norm_one_back(r, carry):
        xhat, rstd = norm_parts(act[r].astype(F32))
        grad = gin_ref[r] + hr[0, r].astype(F32) + hr[1, r].astype(F32)
        carry = carry + jnp.sum(grad * xhat, axis=0, keepdims=True)
        g = grad * gain1
        back = g - jnp.mean(g, axis=-1, keepdims=True) - xhat * jnp.mean(g * xhat, axis=-1, keepdims=True)
        gin_ref[r] = mid[r] + rstd * back
        return carry

    gain1_grad = lax.fori_loop(0, rows, norm_one_back, jnp.zeros((1, depth), F32))

    g_base = take(bits + T)
    GA[0] = jnp.where(row_of == 0, gain1_grad, gain2_grad)

    def ga(k):
        return rc(GA.at[k], GR.at[k], g_base + k, flip(k))

    def gz(i):
        return rc(GA.at[bits], GR.at[bits + z], g_base + bits + i, (b, slab(i)))

    def gains_step(k):
        ga(k).wait()
        GA[k + 1] = GA[k] + GR[k]
        if k + 1 < bits:
            ga(k + 1).start()
        else:
            GR[bits + z] = GA[bits]
            for i in others:
                gz(i).start()

    ga(0).start()
    f2_finish(2)
    f2_finish(1)
    gains_step(0)
    z_finish(0)
    pa2().wait()
    pa3().start()
    gains_step(1)
    f1_finish(0)
    gains_step(2)
    for k in range(3, bits):
        gains_step(k)
    f3_finish(2)
    f3_finish(1)
    f2_finish(0)
    for i in others:
        gz(i).wait()
    total = GR[bits]
    for i in range(1, T):
        total = total + GR[bits + i]
    gains1_ref[...] = total[0:1]
    gains2_ref[...] = total[1:2]
    pa3().wait()
    fp_copy = pltpu.make_async_copy(FP, fp_out, lsem.at[3])
    fp_copy.start()
    f3_finish(0)
    for g in range(3):
        for cp in out_copies(g):
            cp.wait()
    fp_copy.wait()


def per_device(
    tiles,
    batch,
    inputs,
    lengths,
    gain_one,
    qkv_weight,
    out_weight,
    gain_two,
    up_projection_weight,
    down_projection_weight,
    pair_bias,
    cotangent,
):
    tile, rows, depth = inputs.shape
    bits = batch.bit_length() - 1
    channels = qkv_weight.shape[2]
    piece = depth // 8
    window = pair_bias.shape[1]
    strip = tile // 8
    x = jnp.transpose(inputs, (1, 0, 2))
    cot = jnp.transpose(cotangent, (1, 0, 2))
    cut = (2, 2, 2, piece, depth)
    w0 = jnp.concatenate([jnp.transpose(qkv_weight, (0, 2, 1)), out_weight[None]]).reshape(cut)
    w1 = up_projection_weight.reshape(cut)
    w2 = down_projection_weight.reshape(cut)
    n_sems = 256 if bits == 3 else 288
    tokens = (rows, tile, depth)
    T = tiles
    vmem = pl.BlockSpec(memory_space=pltpu.VMEM)
    hbm = pl.BlockSpec(memory_space=pl.ANY)
    blocks = (T, 2, 2, 2, piece, depth)
    upper = max(bits - 3, 1)
    scratch = [
        pltpu.VMEM((2, 2, T, 2, piece, depth), BF),
        pltpu.VMEM(blocks, BF),
        pltpu.VMEM(blocks, BF),
        pltpu.VMEM(blocks, BF),
        pltpu.VMEM(blocks, BF),
        pltpu.VMEM(blocks, BF),
        pltpu.VMEM(blocks, BF),
        pltpu.VMEM((rows, 3, tile, depth), BF),
        pltpu.VMEM((rows, 3, tile, 2 * depth), BF),
        pltpu.VMEM(tokens, F32),
        pltpu.VMEM(tokens, F32),
        pltpu.VMEM(tokens, F32),
        pltpu.VMEM(tokens, F32),
        pltpu.VMEM(tokens, BF),
        pltpu.VMEM(tokens, BF),
        pltpu.VMEM(tokens, BF),
        pltpu.VMEM((rows, tile, 2 * depth), BF),
        pltpu.VMEM(tokens, F32),
        pltpu.VMEM((2,) + tokens, BF),
        pltpu.VMEM((tile, 3 * tile), BF),
        pltpu.VMEM((2, 2, 2, strip, window), BF),
        pltpu.VMEM((2, 2, 2, strip, window), BF),
        pltpu.VMEM((T, 2, 2, 2, strip, window), BF),
        pltpu.VMEM((2, 8, 2 * depth), F32),
        pltpu.VMEM((2, T - 1, 8, 2 * depth), F32),
        pltpu.VMEM((2, 8, 2 * depth), F32),
        pltpu.VMEM((bits + 1, 8, depth), F32),
        pltpu.VMEM((bits + T, 8, depth), F32),
        pltpu.VMEM((upper, strip, window), BF),
        pltpu.SemaphoreType.DMA((n_sems,)),
        pltpu.SemaphoreType.DMA((n_sems,)),
        pltpu.SemaphoreType.DMA((17,)),
        pltpu.SemaphoreType.REGULAR,
        pltpu.SemaphoreType.REGULAR((3, upper)),
    ]
    mixed, grad_inputs, gains1, gains2, fq, fo, f1, f2, pair = pl.pallas_call(
        functools.partial(kernel, T, bits, T * tile, n_sems),
        out_shape=(
            jax.ShapeDtypeStruct(tokens, BF),
            jax.ShapeDtypeStruct(tokens, F32),
            jax.ShapeDtypeStruct((1, depth), F32),
            jax.ShapeDtypeStruct((1, depth), F32),
            jax.ShapeDtypeStruct((3, 2, piece, depth), BF),
            jax.ShapeDtypeStruct((2, piece, depth), BF),
            jax.ShapeDtypeStruct(cut, BF),
            jax.ShapeDtypeStruct(cut, BF),
            jax.ShapeDtypeStruct((T, 2, 2, 2, strip, window), BF),
        ),
        in_specs=[pl.BlockSpec(memory_space=pltpu.SMEM), hbm, vmem, vmem, hbm, hbm, hbm, hbm],
        out_specs=(vmem, vmem, vmem, vmem, hbm, hbm, hbm, hbm, hbm),
        scratch_shapes=scratch,
        compiler_params=pltpu.CompilerParams(
            collective_id=0, has_side_effects=True, vmem_limit_bytes=VMEM_BYTES
        ),
    )(
        lengths,
        x,
        cot,
        jnp.stack([gain_one, gain_two]).astype(F32),
        w0,
        w1,
        w2,
        pair_bias,
    )
    turned = lax.optimization_barrier(jnp.transpose(fq.reshape(3, channels, depth), (0, 2, 1)))
    return (
        jnp.transpose(mixed, (1, 0, 2)),
        jnp.transpose(grad_inputs, (1, 0, 2)),
        gains1.reshape(depth),
        turned.astype(F32),
        fo.reshape(channels, depth).astype(F32),
        gains2.reshape(depth),
        f1.reshape(depth, depth).astype(F32),
        f2.reshape(depth, depth).astype(F32),
        pair.reshape(T * tile, window).astype(F32),
    )


def solution(mesh):
    return jax.shard_map(
        functools.partial(per_device, mesh.shape["tensor"], mesh.shape["batch"]),
        mesh=mesh,
        in_specs=(
            P("tensor", "batch", None),
            P("batch"),
            P(),
            P(None, None, "tensor"),
            P("tensor", None),
            P(),
            P(None, "tensor"),
            P("tensor", None),
            P(),
            P("tensor", "batch", None),
        ),
        out_specs=(
            P("tensor", "batch", None),
            P("tensor", "batch", None),
            P(),
            P(None, None, "tensor"),
            P("tensor", None),
            P(),
            P(None, "tensor"),
            P("tensor", None),
            P(),
        ),
        check_vma=False,
    )
```
